32 devices in a mesh: row: 4 (over z), col: 8 (over y, x, core).
Axes of the slice: x: 2, y: 2, z: 4, core: 2. Of those that a mesh axis runs over, the one named last changes fastest.
Arguments:
- embeddings: float32 [2048, 768], P(('row', 'col'))
- labels: int32 [2048], P(('row', 'col')), may hold values from 0 to 1, as said below
- source_id: int32 [2048], P(('row', 'col')), may hold values from 0 to 2047, as said below
Outputs:
- proof: float32 [2048], P(('row', 'col'))
- mmd_value: float32 [], replicated
The draws below stay inside these ranges and needn't reach their ends.
Inputs may be any that keep to these rules, and one draw needn't show every extreme that they name: `labels`: exactly 1024 samples carry 1. `source_id`: every sample id appears once; at a position of grid block b (positions b * 64 to (b + 1) * 64 - 1) the id's remainder modulo 64, divided by 2 and rounded down, equals b.
All inputs are finite; a program needn't handle non-finite values.
Results may differ from the reference program's by a relative error of at most 0.00007.
Values sent between devices are 32-bit elements; how exact they have to be, the bound alone decides.
No kernel may reach another device: no remote copies, remote signals or barrier semaphores. Data moves between devices by JAX's collectives and lax.ppermute only.
A program may use at most 128 MiB of HBM per device.

```python
import math
import jax
import jax.numpy as jnp
from jax import lax

D = 768
PER_PEER = 2
BLOCKS = 32
SAMP_DEV = 64
SAMPLES = 2048


def label_table(key):
    order = jax.random.permutation(jax.random.fold_in(key, 11), SAMPLES)
    return (order >= SAMPLES // 2).astype(jnp.int32)


def draw_labels(key, part):
    return label_table(key)


def draw_embeddings(key, part):
    labels = label_table(key)
    clusters = SAMPLES // 128
    pick_a = jax.random.randint(jax.random.fold_in(key, 41), (SAMPLES,), 0, clusters)
    pick_b = jax.random.randint(jax.random.fold_in(key, 42), (SAMPLES,), 0, clusters)
    cluster_id = jnp.where(labels == 1, jnp.minimum(pick_a, pick_b), jnp.maximum(pick_a, pick_b))
    sub_id = cluster_id * 4 + jax.random.randint(jax.random.fold_in(key, 43), (SAMPLES,), 0, 4)
    first = jax.random.fold_in(key, 21)
    second = jax.random.fold_in(key, 22)
    third = jax.random.fold_in(key, 23)
    fourth = jax.random.fold_in(key, 24)
    centres = jax.random.normal(first, (clusters, D), jnp.float32)
    subs = jax.random.normal(second, (clusters * 4, D), jnp.float32)
    noise = jax.random.normal(third, (SAMPLES, D), jnp.float32)
    row_scale = jnp.exp(jax.random.uniform(fourth, (SAMPLES, 1), jnp.float32, math.log(0.7), math.log(1.4)))
    result = centres[cluster_id] * math.sqrt(600.0 / D) + subs[sub_id] * math.sqrt(150.0 / D)
    result = result + row_scale * noise * math.sqrt(50.0 / D)
    return result.astype(jnp.float32)


def draw_source_id(key, part):
    block_keys = jax.random.split(jax.random.fold_in(key, 31), BLOCKS)
    shuffles = jax.vmap(lambda one_key: jax.random.permutation(one_key, SAMP_DEV))(block_keys)
    owner_dev = shuffles // PER_PEER
    slot_idx = shuffles % PER_PEER
    block_idx = jnp.arange(BLOCKS, dtype=jnp.int32)[:, None]
    result = owner_dev * SAMP_DEV + block_idx * PER_PEER + slot_idx
    return result.reshape(-1).astype(jnp.int32)


def setup_inputs(seed: int = 0) -> dict:
    keys = jax.random.split(jax.random.key(seed), 4)
    embeddings = draw_embeddings(jax.random.fold_in(keys[3], 71), 0)
    labels = draw_labels(jax.random.fold_in(keys[3], 71), 0)
    source_id = draw_source_id(jax.random.fold_in(keys[3], 71), 0)
    return {"embeddings": embeddings, "labels": labels, "source_id": source_id}


def block_proof(query_rows, query_norm, key_rows, key_norm, key_sign):
    inner_prod = lax.dot_general(query_rows, key_rows, (((1,), (1,)), ((), ())), precision=lax.Precision.HIGHEST, preferred_element_type=jnp.float32)
    sq_dist = query_norm[:, None] + key_norm[None, :] - 2.0 * inner_prod
    kernel = jnp.exp(sq_dist * (-1.0 / 200.0))
    return jnp.dot(kernel, key_sign, precision=lax.Precision.HIGHEST, preferred_element_type=jnp.float32)


def reference(embeddings, labels, source_id):
    set_sign = (1 - 2 * labels).astype(jnp.float32)
    grid_emb = embeddings[source_id.astype(jnp.int32)]
    grid_sign = set_sign[source_id.astype(jnp.int32)]
    sq_norm = jnp.sum(grid_emb * grid_emb, axis=1)
    half_count = SAMPLES // 2
    query_blocks = grid_emb.reshape(-1, 512, D)
    norm_blocks = sq_norm.reshape(-1, 512)

    def one_block(pair):
        return block_proof(pair[0], pair[1], grid_emb, sq_norm, grid_sign)

    sums = lax.map(one_block, (query_blocks, norm_blocks)).reshape(-1)
    proof = sums * (1000.0 / half_count)
    mmd_value = jnp.sum(grid_sign * proof) * (1.0 / half_count)
    return proof, mmd_value
```

```python
import functools

import jax
import jax.numpy as jnp
from jax import lax
from jax.experimental import pallas as pl
from jax.experimental.pallas import tpu as pltpu
from jax.sharding import PartitionSpec as P

LANES = 128
SUBLANES = 8
GROUP_ROWS = 256
PLANES = 4
CORES = 2
ROUND_A = {2: 0, 3: 1, 1: 2, 0: 3}
ROUND_B = {0: 1, 3: 2, 1: 0, 2: 3}
CROSSING = (1, 2)
FAR_BLOCKS = 3
MIB = 1024 * 1024
NT_DIMS = (((1,), (1,)), ((), ()))
NN_DIMS = (((1,), (0,)), ((), ()))


def int_div(value, divisor):
    if divisor & (divisor - 1) == 0:
        return lax.shift_right_logical(value, divisor.bit_length() - 1)
    return value // divisor


def int_mod(value, divisor):
    if divisor & (divisor - 1) == 0:
        return value & (divisor - 1)
    return value % divisor


class Layout:
    def __init__(self, row_count, col_count):
        self.core_in_row = row_count == PLANES * CORES
        self.places = col_count if self.core_in_row else col_count // CORES
        self.devices = row_count * col_count

    def flat(self, plane, place, core):
        if self.core_in_row:
            return (plane * CORES + core) * self.places + place
        return (plane * self.places + place) * CORES + core

    def parts(self, flat):
        if self.core_in_row:
            place, rest = int_mod(flat, self.places), int_div(flat, self.places)
            return int_div(rest, CORES), place, int_mod(rest, CORES)
        core, rest = int_mod(flat, CORES), int_div(flat, CORES)
        return int_div(rest, self.places), int_mod(rest, self.places), core

    def here(self):
        row, col = lax.axis_index("row"), lax.axis_index("col")
        if self.core_in_row:
            return int_div(row, CORES), col, int_mod(row, CORES)
        return row, int_div(col, CORES), int_mod(col, CORES)

    def pairs(self, target):
        result = []
        for plane in range(PLANES):
            for place in range(self.places):
                for core in range(CORES):
                    goal = target(plane, place, core)
                    result.append((self.flat(plane, place, core), self.flat(*goal)))
        return sorted(result)


def split2(value):
    high = value.astype(jnp.bfloat16)
    return high, (value - high.astype(jnp.float32)).astype(jnp.bfloat16)


def split3(value):
    high = value.astype(jnp.bfloat16)
    rest = value - high.astype(jnp.float32)
    mid = rest.astype(jnp.bfloat16)
    low = (rest - mid.astype(jnp.float32)).astype(jnp.bfloat16)
    return high, mid, low


def bf16_dot(left, right, dims):
    return lax.dot_general(left, right, dims, preferred_element_type=jnp.float32)


def pack_kernel(emb_ref, label_ref, id_ref, out_ref, id_out_ref):
    samples, width = emb_ref.shape
    id_out_ref[...] = id_ref[...]
    emb = emb_ref[...]
    norm = lax.dot_general(
        jnp.ones((SUBLANES, width), jnp.float32),
        emb * emb,
        NT_DIMS,
        precision=lax.Precision.HIGHEST,
        preferred_element_type=jnp.float32,
    )
    sign = (1 - 2 * label_ref[...]).astype(jnp.float32)
    for chunk in range(width // LANES):
        out_ref[pl.ds(chunk * samples, samples), :] = emb[:, chunk * LANES : (chunk + 1) * LANES]
    base = samples * (width // LANES)
    row = lax.broadcasted_iota(jnp.int32, (SUBLANES, samples), 0)
    both = jnp.where(row == 0, sign, norm)
    for start in range(0, samples, LANES):
        lanes = min(LANES, samples - start)
        place = base + start // LANES * SUBLANES
        if lanes < LANES:
            out_ref[pl.ds(place, SUBLANES), :] = jnp.zeros((SUBLANES, LANES), jnp.float32)
        out_ref[pl.ds(place, SUBLANES), pl.ds(0, lanes)] = both[:, start : start + lanes]


def stage(ref, scratch, start, samples, chunks):
    for chunk in range(chunks):
        value = ref[pl.ds(chunk * samples, samples), :]
        for part, piece in zip(scratch, split2(value)):
            part[pl.ds(start, samples), pl.ds(chunk * LANES, LANES)] = piece


def tail_rows(refs, samples, chunks):
    pieces = []
    for ref in refs:
        for start in range(0, samples, LANES):
            lanes = min(LANES, samples - start)
            place = samples * chunks + start // LANES * SUBLANES
            pieces.append(ref[pl.ds(place, SUBLANES), pl.ds(0, lanes)])
    return jnp.concatenate(pieces, axis=1)


def main_kernel(samples, chunks, layout, *refs):
    places = layout.places
    queries = refs[:places]
    keys = (refs[0],) + refs[places : places + 4]
    out_ref = refs[places + 4]
    key_parts = refs[places + 5 : places + 7]
    query_parts = refs[places + 7 : places + 9]
    tail_ref = refs[places + 9]
    _, me_place, me_core = layout.here()
    rows = places * samples
    group = min(GROUP_ROWS, rows)
    blocks = group // samples
    near = CORES * samples
    for place, ref in enumerate(keys):
        stage(ref, key_parts, place * samples, samples, chunks)
    for place, ref in enumerate(queries):
        stage(ref, query_parts, place * samples, samples, chunks)
    key_tail = tail_rows(keys, samples, chunks)
    key_sign, key_norm = key_tail[0:1, :], key_tail[1:2, :]
    tail_ref[...] = jnp.transpose(tail_rows(queries, samples, chunks))
    lane = lax.broadcasted_iota(jnp.int32, (samples, LANES), 1)

    def one_group(index, carry):
        result, total, column = carry
        start = pl.multiple_of(index * group, group)
        high, mid = (part[pl.ds(start, group), :] for part in query_parts)
        key_high, key_mid = (part[...] for part in key_parts)
        inner = bf16_dot(mid, key_mid, NT_DIMS)
        inner = inner + (bf16_dot(high, key_mid, NT_DIMS) + bf16_dot(mid, key_high, NT_DIMS))
        inner = inner + bf16_dot(high, key_high, NT_DIMS)
        sign = tail_ref[pl.ds(start, group), 0:1]
        norm = tail_ref[pl.ds(start, group), 1:2]
        sq_dist = norm + key_norm - 2.0 * inner
        kernel = jnp.exp(sq_dist * (-1.0 / 200.0))
        signed = kernel * key_sign
        near_sums = jnp.sum(signed[:, :near], axis=1, keepdims=True)
        far_sums = jnp.sum(signed[:, near:], axis=1, keepdims=True)
        sums = near_sums + far_sums
        total = total + jnp.sum(sign * (sums + far_sums), axis=0, keepdims=True)
        column = column + jnp.sum(kernel[:, near:] * sign, axis=0, keepdims=True)
        for place in range(blocks):
            owner = me_place ^ (index * blocks + place)
            result = jnp.where(
                lane == owner, sums[place * samples : (place + 1) * samples, :], result
            )
        return result, total, column

    carry = (
        jnp.zeros((samples, LANES), jnp.float32),
        jnp.zeros((1, 1), jnp.float32),
        jnp.zeros((1, FAR_BLOCKS * samples), jnp.float32),
    )
    if rows == group:
        carry = one_group(0, carry)
    else:
        carry = lax.fori_loop(0, rows // group, one_group, carry)
    result, total, column = carry
    column = jnp.concatenate([column, jnp.zeros((1, samples), jnp.float32)], axis=1)
    column = jnp.transpose(jnp.broadcast_to(column, (SUBLANES, (FAR_BLOCKS + 1) * samples)))
    for place, offset in enumerate((me_core, 1 - me_core, 2)):
        result = jnp.where(
            lane == places + offset, column[place * samples : (place + 1) * samples, 0:1], result
        )
    out_ref[...] = jnp.where(lane == places + 4, total, result)


def last_kernel(layout, samples, per_peer, factor, half_count, got_ref, id_ref, proof_ref, mmd_ref):
    got = got_ref[...]
    ids = id_ref[...]
    places = layout.places
    plane, place, core = layout.parts(int_div(ids, samples))
    slot = int_mod(ids, per_peer)
    targets = jnp.concatenate(
        [place, places + core, jnp.full(core.shape, places + 2, jnp.int32)], axis=1
    )
    lane_of = lax.broadcasted_iota(jnp.int32, (LANES, 3 * samples), 0)
    picks = jnp.where(lane_of == targets, 1.0, 0.0).astype(jnp.bfloat16)
    high, mid, low = split3(got)
    picked = bf16_dot(high, picks, NN_DIMS) + (
        bf16_dot(mid, picks, NN_DIMS) + bf16_dot(low, picks, NN_DIMS)
    )
    row = lax.broadcasted_iota(jnp.int32, (samples, samples), 0)
    src_plane, src_place, src_core = layout.parts(int_div(row, per_peer))
    right_slot = int_mod(row, per_peer) == slot
    keep_row = right_slot & (src_plane == plane) & (src_core == core)
    right_place = right_slot & (src_place == place)

    def sent_to(table):
        goal = jnp.full(plane.shape, -1, jnp.int32)
        for source, target in table.items():
            goal = jnp.where(plane == source, target, goal)
        return goal

    keep_a = right_place & (src_plane == sent_to(ROUND_A))
    crossing = (plane == CROSSING[0]) | (plane == CROSSING[1])
    keep_b = right_place & (src_plane == sent_to(ROUND_B))
    keep_b = keep_b & (src_core == jnp.where(crossing, 1 - core, core))
    sums = jnp.where(keep_row, picked[:, :samples], 0.0)
    sums = sums + jnp.where(keep_a, picked[:, samples : 2 * samples], 0.0)
    sums = sums + jnp.where(keep_b, picked[:, 2 * samples :], 0.0)
    proof_ref[...] = jnp.sum(sums, axis=0, keepdims=True) * factor
    row = lax.broadcasted_iota(jnp.int32, (samples, LANES), 0)
    lane = lax.broadcasted_iota(jnp.int32, (samples, LANES), 1)
    is_total = (lane == places + 4) & (int_mod(row, per_peer) == 0)
    total = jnp.sum(jnp.where(is_total, got, 0.0), axis=(0, 1), keepdims=True)
    mmd_ref[...] = total * factor * (1.0 / half_count)


def in_vmem(array):
    return pltpu.with_memory_space_constraint(array, pltpu.VMEM)


def in_hbm(array):
    return pltpu.with_memory_space_constraint(array, pltpu.HBM)


def vmem_specs(count):
    return [pl.BlockSpec(memory_space=pltpu.VMEM)] * count


def local(embeddings, labels, source_id):
    layout = Layout(lax.axis_size("row"), lax.axis_size("col"))
    places = layout.places
    samples, width = embeddings.shape
    chunks = width // LANES
    per_peer = samples // layout.devices
    half_count = samples * layout.devices // 2
    factor = 1000.0 / half_count
    tiles = -(-samples // LANES)
    pack_rows = samples * chunks + tiles * SUBLANES
    key_rows = (CORES + FAR_BLOCKS) * samples
    query_rows = places * samples
    block_bytes = pack_rows * LANES * 4
    work_bytes = (key_rows + query_rows) * width * 6 + 8 * GROUP_ROWS * key_rows * 4
    params = pltpu.CompilerParams(vmem_limit_bytes=work_bytes + 4 * MIB)

    packed, ids = pl.pallas_call(
        pack_kernel,
        out_shape=(
            pltpu.VMEM((pack_rows, LANES), jnp.float32),
            pltpu.VMEM((1, samples), jnp.int32),
        ),
        in_specs=vmem_specs(3),
        out_specs=tuple(vmem_specs(2)),
        compiler_params=pltpu.CompilerParams(vmem_limit_bytes=4 * block_bytes + 4 * MIB),
        name="pack_block",
    )(
        in_hbm(embeddings),
        in_hbm(labels.reshape(1, samples)),
        in_hbm(source_id.reshape(1, samples)),
    )

    def send(block, target):
        return lax.ppermute(block, ("row", "col"), layout.pairs(target))

    def round_a(plane, place, core):
        return (ROUND_A[plane], place, core)

    def round_b(plane, place, core):
        return (ROUND_B[plane], place, 1 - core if plane in CROSSING else core)

    def to_place(step):
        return lambda plane, place, core: (plane, place ^ step, core)

    def to_core(plane, place, core):
        return (plane, place, 1 - core)

    in_plane = [send(packed, to_place(step)) for step in range(1, places)]
    far_b = send(packed, round_b)
    far_a = send(packed, round_a)
    far_a_other = send(far_a, to_core)
    late, *_ = lax.optimization_barrier((packed, in_plane[-1], far_a))
    near = send(late, to_core)

    blocks = [packed, *in_plane, near, far_a, far_a_other, far_b]
    partial = pl.pallas_call(
        functools.partial(main_kernel, samples, chunks, layout),
        out_shape=pltpu.VMEM((samples, LANES), jnp.float32),
        in_specs=vmem_specs(len(blocks)),
        out_specs=pl.BlockSpec(memory_space=pltpu.VMEM),
        scratch_shapes=[pltpu.VMEM((key_rows, width), jnp.bfloat16)] * 2
        + [pltpu.VMEM((query_rows, width), jnp.bfloat16)] * 2
        + [pltpu.VMEM((query_rows, SUBLANES), jnp.float32)],
        compiler_params=params,
        name="kernel_sums",
    )(*[in_vmem(block) for block in blocks])

    got = lax.all_to_all(partial, ("row", "col"), split_axis=0, concat_axis=0, tiled=True)

    proof, mmd = pl.pallas_call(
        functools.partial(last_kernel, layout, samples, per_peer, factor, half_count),
        out_shape=(
            jax.ShapeDtypeStruct((1, samples), jnp.float32),
            jax.ShapeDtypeStruct((1, 1), jnp.float32),
        ),
        in_specs=vmem_specs(2),
        out_specs=tuple(vmem_specs(2)),
        compiler_params=pltpu.CompilerParams(vmem_limit_bytes=16 * MIB),
        name="pick_proof",
    )(in_vmem(got), in_vmem(ids))
    return proof.reshape(samples), mmd.reshape(())


def solution(mesh):
    return jax.shard_map(
        local,
        mesh=mesh,
        in_specs=(P(("row", "col"), None), P(("row", "col")), P(("row", "col"))),
        out_specs=(P(("row", "col")), P()),
        check_vma=False,
    )
```

```python
import functools

import jax
import jax.numpy as jnp
from jax import lax
from jax.experimental import pallas as pl
from jax.experimental.pallas import tpu as pltpu
from jax.sharding import PartitionSpec as P

LANES = 128
SUBLANES = 8
GROUP_ROWS = 256
PLANES = 4
CORES = 2
ROUND_A = {2: 0, 3: 1, 1: 2, 0: 3}
ROUND_B = {0: 1, 3: 2, 1: 0, 2: 3}
CROSSING = (1, 2)
FAR_BLOCKS = 3
MIB = 1024 * 1024
NT_DIMS = (((1,), (1,)), ((), ()))
NN_DIMS = (((1,), (0,)), ((), ()))


def int_div(value, divisor):
    if divisor & (divisor - 1) == 0:
        return lax.shift_right_logical(value, divisor.bit_length() - 1)
    return value // divisor


def int_mod(value, divisor):
    if divisor & (divisor - 1) == 0:
        return value & (divisor - 1)
    return value % divisor


class Layout:
    def __init__(self, row_count, col_count):
        self.core_in_row = row_count == PLANES * CORES
        self.places = col_count if self.core_in_row else col_count // CORES
        self.devices = row_count * col_count

    def flat(self, plane, place, core):
        if self.core_in_row:
            return (plane * CORES + core) * self.places + place
        return (plane * self.places + place) * CORES + core

    def parts(self, flat):
        if self.core_in_row:
            place, rest = int_mod(flat, self.places), int_div(flat, self.places)
            return int_div(rest, CORES), place, int_mod(rest, CORES)
        core, rest = int_mod(flat, CORES), int_div(flat, CORES)
        return int_div(rest, self.places), int_mod(rest, self.places), core

    def here(self):
        row, col = lax.axis_index("row"), lax.axis_index("col")
        if self.core_in_row:
            return int_div(row, CORES), col, int_mod(row, CORES)
        return row, int_div(col, CORES), int_mod(col, CORES)

    def pairs(self, target):
        result = []
        for plane in range(PLANES):
            for place in range(self.places):
                for core in range(CORES):
                    goal = target(plane, place, core)
                    result.append((self.flat(plane, place, core), self.flat(*goal)))
        return sorted(result)


def split2(value):
    high = value.astype(jnp.bfloat16)
    return high, (value - high.astype(jnp.float32)).astype(jnp.bfloat16)


def split3(value):
    high = value.astype(jnp.bfloat16)
    rest = value - high.astype(jnp.float32)
    mid = rest.astype(jnp.bfloat16)
    low = (rest - mid.astype(jnp.float32)).astype(jnp.bfloat16)
    return high, mid, low


def bf16_dot(left, right, dims):
    return lax.dot_general(left, right, dims, preferred_element_type=jnp.float32)


def pack_kernel(emb_ref, label_ref, id_ref, out_ref, id_out_ref):
    samples, width = emb_ref.shape
    id_out_ref[...] = id_ref[...]
    emb = emb_ref[...]
    norm = lax.dot_general(
        jnp.ones((SUBLANES, width), jnp.float32),
        emb * emb,
        NT_DIMS,
        precision=lax.Precision.HIGHEST,
        preferred_element_type=jnp.float32,
    )
    sign = (1 - 2 * label_ref[...]).astype(jnp.float32)
    for chunk in range(width // LANES):
        out_ref[pl.ds(chunk * samples, samples), :] = emb[:, chunk * LANES : (chunk + 1) * LANES]
    base = samples * (width // LANES)
    row = lax.broadcasted_iota(jnp.int32, (SUBLANES, samples), 0)
    both = jnp.where(row == 0, sign, norm)
    for start in range(0, samples, LANES):
        lanes = min(LANES, samples - start)
        place = base + start // LANES * SUBLANES
        if lanes < LANES:
            out_ref[pl.ds(place, SUBLANES), :] = jnp.zeros((SUBLANES, LANES), jnp.float32)
        out_ref[pl.ds(place, SUBLANES), pl.ds(0, lanes)] = both[:, start : start + lanes]


def stage(ref, scratch, start, middle, samples, chunks):
    for chunk in range(chunks):
        value = ref[pl.ds(chunk * samples, samples), :]
        for offset, piece in zip((0, middle), split2(value)):
            scratch[pl.ds(offset + start, samples), pl.ds(chunk * LANES, LANES)] = piece


def tail_rows(refs, samples, chunks):
    pieces = []
    for ref in refs:
        for start in range(0, samples, LANES):
            lanes = min(LANES, samples - start)
            place = samples * chunks + start // LANES * SUBLANES
            pieces.append(ref[pl.ds(place, SUBLANES), pl.ds(0, lanes)])
    return jnp.concatenate(pieces, axis=1)


def as_columns(rows):
    count = rows.shape[1]
    fill = -count % LANES
    if fill:
        rows = jnp.concatenate([rows, jnp.zeros((SUBLANES, fill), jnp.float32)], axis=1)
    return jnp.transpose(rows)[:count]


def main_kernel(samples, chunks, layout, *refs):
    places = layout.places
    queries = refs[:places]
    keys = (refs[0],) + refs[places : places + 4]
    out_ref, key_parts, query_parts, tail_ref = refs[places + 4 :]
    _, me_place, me_core = layout.here()
    rows = places * samples
    key_rows = len(keys) * samples
    group = min(GROUP_ROWS, rows)
    blocks = group // samples
    near = CORES * samples
    for place, ref in enumerate(queries):
        stage(ref, query_parts, place * samples, rows, samples, chunks)
    for place, ref in enumerate(keys):
        stage(ref, key_parts, place * samples, key_rows, samples, chunks)
    key_tail = as_columns(tail_rows(keys, samples, chunks))
    key_sign, key_norm = key_tail[:, 0:1], key_tail[:, 1:2]
    tail_ref[...] = tail_rows(queries, samples, chunks)
    lane = lax.broadcasted_iota(jnp.int32, (samples, LANES), 1)

    def one_group(index, carry):
        result, total, column = carry
        start = pl.multiple_of(index * group, group)
        both = key_parts[...]
        by_high = bf16_dot(both, query_parts[pl.ds(start, group), :], NT_DIMS)
        by_mid = bf16_dot(both, query_parts[pl.ds(rows + start, group), :], NT_DIMS)
        inner = by_high[:key_rows] + (by_high[key_rows:] + by_mid[:key_rows] + by_mid[key_rows:])
        sign = tail_ref[0:1, pl.ds(start, group)]
        norm = tail_ref[1:2, pl.ds(start, group)]
        sq_dist = norm + key_norm - 2.0 * inner
        kernel = jnp.exp(sq_dist * (-1.0 / 200.0))
        signed = kernel * key_sign
        near_sums = jnp.sum(signed[:near], axis=0, keepdims=True)
        far_sums = jnp.sum(signed[near:], axis=0, keepdims=True)
        sums = near_sums + far_sums
        total = total + jnp.sum(sign * (sums + far_sums), axis=1, keepdims=True)
        column = column + jnp.sum(kernel[near:] * sign, axis=1, keepdims=True)
        sums = as_columns(jnp.broadcast_to(sums, (SUBLANES, group)))
        for place in range(blocks):
            owner = me_place ^ (index * blocks + place)
            result = jnp.where(
                lane == owner, sums[place * samples : (place + 1) * samples, 0:1], result
            )
        return result, total, column

    carry = (
        jnp.zeros((samples, LANES), jnp.float32),
        jnp.zeros((1, 1), jnp.float32),
        jnp.zeros((FAR_BLOCKS * samples, 1), jnp.float32),
    )
    if rows == group:
        carry = one_group(0, carry)
    else:
        carry = lax.fori_loop(0, rows // group, one_group, carry)
    result, total, column = carry
    for place, offset in enumerate((me_core, 1 - me_core, 2)):
        result = jnp.where(
            lane == places + offset, column[place * samples : (place + 1) * samples], result
        )
    out_ref[...] = jnp.where(lane == places + 4, total, result)


def last_kernel(layout, samples, per_peer, factor, half_count, got_ref, id_ref, proof_ref, mmd_ref):
    got = got_ref[...]
    ids = id_ref[...]
    places = layout.places
    plane, place, core = layout.parts(int_div(ids, samples))
    slot = int_mod(ids, per_peer)
    targets = jnp.concatenate(
        [place, places + core, jnp.full(core.shape, places + 2, jnp.int32)], axis=1
    )
    lane_of = lax.broadcasted_iota(jnp.int32, (LANES, 3 * samples), 0)
    picks = jnp.where(lane_of == targets, 1.0, 0.0).astype(jnp.bfloat16)
    high, mid, low = split3(got)
    picked = bf16_dot(high, picks, NN_DIMS) + (
        bf16_dot(mid, picks, NN_DIMS) + bf16_dot(low, picks, NN_DIMS)
    )
    row = lax.broadcasted_iota(jnp.int32, (samples, samples), 0)
    src_plane, src_place, src_core = layout.parts(int_div(row, per_peer))
    right_slot = int_mod(row, per_peer) == slot
    keep_row = right_slot & (src_plane == plane) & (src_core == core)
    right_place = right_slot & (src_place == place)

    def sent_to(table):
        goal = jnp.full(plane.shape, -1, jnp.int32)
        for source, target in table.items():
            goal = jnp.where(plane == source, target, goal)
        return goal

    keep_a = right_place & (src_plane == sent_to(ROUND_A))
    crossing = (plane == CROSSING[0]) | (plane == CROSSING[1])
    keep_b = right_place & (src_plane == sent_to(ROUND_B))
    keep_b = keep_b & (src_core == jnp.where(crossing, 1 - core, core))
    sums = jnp.where(keep_row, picked[:, :samples], 0.0)
    sums = sums + jnp.where(keep_a, picked[:, samples : 2 * samples], 0.0)
    sums = sums + jnp.where(keep_b, picked[:, 2 * samples :], 0.0)
    proof_ref[...] = jnp.sum(sums, axis=0, keepdims=True) * factor
    row = lax.broadcasted_iota(jnp.int32, (samples, LANES), 0)
    lane = lax.broadcasted_iota(jnp.int32, (samples, LANES), 1)
    is_total = (lane == places + 4) & (int_mod(row, per_peer) == 0)
    total = jnp.sum(jnp.where(is_total, got, 0.0), axis=(0, 1), keepdims=True)
    mmd_ref[...] = total * factor * (1.0 / half_count)


def in_vmem(array):
    return pltpu.with_memory_space_constraint(array, pltpu.VMEM)


def in_hbm(array):
    return pltpu.with_memory_space_constraint(array, pltpu.HBM)


def vmem_specs(count):
    return [pl.BlockSpec(memory_space=pltpu.VMEM)] * count


def local(embeddings, labels, source_id):
    layout = Layout(lax.axis_size("row"), lax.axis_size("col"))
    places = layout.places
    samples, width = embeddings.shape
    chunks = width // LANES
    per_peer = samples // layout.devices
    half_count = samples * layout.devices // 2
    factor = 1000.0 / half_count
    tiles = -(-samples // LANES)
    pack_rows = samples * chunks + tiles * SUBLANES
    key_rows = (CORES + FAR_BLOCKS) * samples
    query_rows = places * samples
    block_bytes = pack_rows * LANES * 4
    work_bytes = (key_rows + query_rows) * width * 6 + 8 * GROUP_ROWS * key_rows * 4
    params = pltpu.CompilerParams(vmem_limit_bytes=work_bytes + 4 * MIB)

    packed, ids = pl.pallas_call(
        pack_kernel,
        out_shape=(
            pltpu.VMEM((pack_rows, LANES), jnp.float32),
            pltpu.VMEM((1, samples), jnp.int32),
        ),
        in_specs=vmem_specs(3),
        out_specs=tuple(vmem_specs(2)),
        compiler_params=pltpu.CompilerParams(vmem_limit_bytes=4 * block_bytes + 4 * MIB),
        name="pack_block",
    )(
        in_hbm(embeddings),
        in_hbm(labels.reshape(1, samples)),
        in_hbm(source_id.reshape(1, samples)),
    )

    def send(block, target):
        return lax.ppermute(block, ("row", "col"), layout.pairs(target))

    def round_a(plane, place, core):
        return (ROUND_A[plane], place, core)

    def round_b(plane, place, core):
        return (ROUND_B[plane], place, 1 - core if plane in CROSSING else core)

    def to_place(step):
        return lambda plane, place, core: (plane, place ^ step, core)

    def to_core(plane, place, core):
        return (plane, place, 1 - core)

    in_plane = [send(packed, to_place(step)) for step in range(1, places)]
    far_b = send(packed, round_b)
    far_a = send(packed, round_a)
    far_a_other = send(far_a, to_core)
    late, *_ = lax.optimization_barrier((packed, in_plane[-1], far_a))
    near = send(late, to_core)

    blocks = [packed, *in_plane, near, far_a, far_a_other, far_b]
    partial = pl.pallas_call(
        functools.partial(main_kernel, samples, chunks, layout),
        out_shape=pltpu.VMEM((samples, LANES), jnp.float32),
        in_specs=vmem_specs(len(blocks)),
        out_specs=pl.BlockSpec(memory_space=pltpu.VMEM),
        scratch_shapes=[
            pltpu.VMEM((2 * key_rows, width), jnp.bfloat16),
            pltpu.VMEM((2 * query_rows, width), jnp.bfloat16),
            pltpu.VMEM((SUBLANES, query_rows), jnp.float32),
        ],
        compiler_params=params,
        name="kernel_sums",
    )(*[in_vmem(block) for block in blocks])

    got = lax.all_to_all(partial, ("row", "col"), split_axis=0, concat_axis=0, tiled=True)

    proof, mmd = pl.pallas_call(
        functools.partial(last_kernel, layout, samples, per_peer, factor, half_count),
        out_shape=(
            jax.ShapeDtypeStruct((1, samples), jnp.float32),
            jax.ShapeDtypeStruct((1, 1), jnp.float32),
        ),
        in_specs=vmem_specs(2),
        out_specs=tuple(vmem_specs(2)),
        compiler_params=pltpu.CompilerParams(vmem_limit_bytes=16 * MIB),
        name="pick_proof",
    )(in_vmem(got), in_vmem(ids))
    return proof.reshape(samples), mmd.reshape(())


def solution(mesh):
    return jax.shard_map(
        local,
        mesh=mesh,
        in_specs=(P(("row", "col"), None), P(("row", "col")), P(("row", "col"))),
        out_specs=(P(("row", "col")), P()),
        check_vma=False,
    )
```

```python
import functools

import jax
import jax.numpy as jnp
from jax import lax
from jax.experimental import pallas as pl
from jax.experimental.pallas import tpu as pltpu
from jax.sharding import PartitionSpec as P

LANES = 128
SUBLANES = 8
GROUP_ROWS = 256
PLANES = 4
CORES = 2
ROUND_A = {2: 0, 3: 1, 1: 2, 0: 3}
ROUND_B = {0: 1, 3: 2, 1: 0, 2: 3}
CROSSING = (1, 2)
FAR_BLOCKS = 3
MIB = 1024 * 1024
NT_DIMS = (((1,), (1,)), ((), ()))
NN_DIMS = (((1,), (0,)), ((), ()))


def int_div(value, divisor):
    if divisor & (divisor - 1) == 0:
        return lax.shift_right_logical(value, divisor.bit_length() - 1)
    return value // divisor


def int_mod(value, divisor):
    if divisor & (divisor - 1) == 0:
        return value & (divisor - 1)
    return value % divisor


class Layout:
    def __init__(self, row_count, col_count):
        self.core_in_row = row_count == PLANES * CORES
        self.places = col_count if self.core_in_row else col_count // CORES
        self.devices = row_count * col_count

    def flat(self, plane, place, core):
        if self.core_in_row:
            return (plane * CORES + core) * self.places + place
        return (plane * self.places + place) * CORES + core

    def parts(self, flat):
        if self.core_in_row:
            place, rest = int_mod(flat, self.places), int_div(flat, self.places)
            return int_div(rest, CORES), place, int_mod(rest, CORES)
        core, rest = int_mod(flat, CORES), int_div(flat, CORES)
        return int_div(rest, self.places), int_mod(rest, self.places), core

    def here(self):
        row, col = lax.axis_index("row"), lax.axis_index("col")
        if self.core_in_row:
            return int_div(row, CORES), col, int_mod(row, CORES)
        return row, int_div(col, CORES), int_mod(col, CORES)

    def pairs(self, target):
        result = []
        for plane in range(PLANES):
            for place in range(self.places):
                for core in range(CORES):
                    goal = target(plane, place, core)
                    result.append((self.flat(plane, place, core), self.flat(*goal)))
        return sorted(result)


def split2(value):
    high = value.astype(jnp.bfloat16)
    return high, (value - high.astype(jnp.float32)).astype(jnp.bfloat16)


def split3(value):
    high = value.astype(jnp.bfloat16)
    rest = value - high.astype(jnp.float32)
    mid = rest.astype(jnp.bfloat16)
    low = (rest - mid.astype(jnp.float32)).astype(jnp.bfloat16)
    return high, mid, low


def bf16_dot(left, right, dims):
    return lax.dot_general(left, right, dims, preferred_element_type=jnp.float32)


def pack_kernel(emb_ref, label_ref, id_ref, out_ref, id_out_ref):
    samples, width = emb_ref.shape
    id_out_ref[...] = id_ref[...]
    emb = emb_ref[...]
    norm = lax.dot_general(
        jnp.ones((SUBLANES, width), jnp.float32),
        emb * emb,
        NT_DIMS,
        precision=lax.Precision.HIGHEST,
        preferred_element_type=jnp.float32,
    )
    sign = (1 - 2 * label_ref[...]).astype(jnp.float32)
    for chunk in range(width // LANES):
        out_ref[pl.ds(chunk * samples, samples), :] = emb[:, chunk * LANES : (chunk + 1) * LANES]
    base = samples * (width // LANES)
    row = lax.broadcasted_iota(jnp.int32, (SUBLANES, samples), 0)
    both = jnp.where(row == 0, sign, norm)
    for start in range(0, samples, LANES):
        lanes = min(LANES, samples - start)
        place = base + start // LANES * SUBLANES
        if lanes < LANES:
            out_ref[pl.ds(place, SUBLANES), :] = jnp.zeros((SUBLANES, LANES), jnp.float32)
        out_ref[pl.ds(place, SUBLANES), pl.ds(0, lanes)] = both[:, start : start + lanes]


def stage(ref, scratch, start, middle, samples, chunks):
    for chunk in range(chunks):
        value = ref[pl.ds(chunk * samples, samples), :]
        for offset, piece in zip((0, middle), split2(value)):
            scratch[pl.ds(offset + start, samples), pl.ds(chunk * LANES, LANES)] = piece


def tail_rows(refs, samples, chunks):
    pieces = []
    for ref in refs:
        for start in range(0, samples, LANES):
            lanes = min(LANES, samples - start)
            place = samples * chunks + start // LANES * SUBLANES
            pieces.append(ref[pl.ds(place, SUBLANES), pl.ds(0, lanes)])
    return jnp.concatenate(pieces, axis=1)


def as_columns(rows):
    count = rows.shape[1]
    fill = -count % LANES
    if fill:
        rows = jnp.concatenate([rows, jnp.zeros((SUBLANES, fill), jnp.float32)], axis=1)
    return jnp.transpose(rows)[:count]


def main_kernel(samples, chunks, layout, *refs):
    places = layout.places
    queries = refs[:places]
    keys = (refs[0],) + refs[places : places + 4]
    out_ref, key_parts, query_parts, tail_ref = refs[places + 4 :]
    _, me_place, me_core = layout.here()
    rows = places * samples
    key_rows = len(keys) * samples
    group = min(GROUP_ROWS, rows)
    blocks = group // samples
    near = CORES * samples
    for place, ref in enumerate(queries):
        stage(ref, query_parts, place * samples, rows, samples, chunks)
    for place, ref in enumerate(keys):
        stage(ref, key_parts, place * samples, key_rows, samples, chunks)
    key_tail = as_columns(tail_rows(keys, samples, chunks))
    key_sign, key_norm = key_tail[:, 0:1], key_tail[:, 1:2]
    tail_ref[...] = tail_rows(queries, samples, chunks)
    lane = lax.broadcasted_iota(jnp.int32, (samples, LANES), 1)

    def one_group(index, carry):
        result, total, column = carry
        start = pl.multiple_of(index * group, group)
        both = key_parts[...]
        by_high = bf16_dot(both, query_parts[pl.ds(start, group), :], NT_DIMS)
        by_mid = bf16_dot(both, query_parts[pl.ds(rows + start, group), :], NT_DIMS)
        inner = by_high[:key_rows] + (by_high[key_rows:] + by_mid[:key_rows] + by_mid[key_rows:])
        sign = tail_ref[0:1, pl.ds(start, group)]
        norm = tail_ref[1:2, pl.ds(start, group)]
        sq_dist = norm + key_norm - 2.0 * inner
        kernel = jnp.exp(sq_dist * (-1.0 / 200.0))
        signed = kernel * key_sign
        near_sums = jnp.sum(signed[:near], axis=0, keepdims=True)
        far_sums = jnp.sum(signed[near:], axis=0, keepdims=True)
        sums = near_sums + far_sums
        total = total + jnp.sum(sign * (sums + far_sums), axis=1, keepdims=True)
        column = column + jnp.sum(kernel[near:] * sign, axis=1, keepdims=True)
        sums = as_columns(jnp.broadcast_to(sums, (SUBLANES, group)))
        for place in range(blocks):
            owner = me_place ^ (index * blocks + place)
            result = jnp.where(
                lane == owner, sums[place * samples : (place + 1) * samples, 0:1], result
            )
        return result, total, column

    carry = (
        jnp.zeros((samples, LANES), jnp.float32),
        jnp.zeros((1, 1), jnp.float32),
        jnp.zeros((FAR_BLOCKS * samples, 1), jnp.float32),
    )
    if rows == group:
        carry = one_group(0, carry)
    else:
        carry = lax.fori_loop(0, rows // group, one_group, carry)
    result, total, column = carry
    for place, offset in enumerate((me_core, 1 - me_core, 2)):
        result = jnp.where(
            lane == places + offset, column[place * samples : (place + 1) * samples], result
        )
    out_ref[...] = jnp.where(lane == places + 4, total, result)


def last_kernel(layout, samples, per_peer, factor, half_count, got_ref, id_ref, proof_ref, mmd_ref):
    got = got_ref[...]
    ids = id_ref[...]
    places = layout.places
    plane, place, core = layout.parts(int_div(ids, samples))
    slot = int_mod(ids, per_peer)
    targets = jnp.concatenate(
        [place, places + core, jnp.full(core.shape, places + 2, jnp.int32)], axis=1
    )
    lane_of = lax.broadcasted_iota(jnp.int32, (LANES, 3 * samples), 0)
    picks = jnp.where(lane_of == targets, 1.0, 0.0).astype(jnp.bfloat16)
    high, mid, low = split3(got)
    picked = bf16_dot(high, picks, NN_DIMS) + (
        bf16_dot(mid, picks, NN_DIMS) + bf16_dot(low, picks, NN_DIMS)
    )
    row = lax.broadcasted_iota(jnp.int32, (samples, samples), 0)
    src_plane, src_place, src_core = layout.parts(int_div(row, per_peer))
    right_slot = int_mod(row, per_peer) == slot
    keep_row = right_slot & (src_plane == plane) & (src_core == core)
    right_place = right_slot & (src_place == place)

    def sent_to(table):
        goal = jnp.full(plane.shape, -1, jnp.int32)
        for source, target in table.items():
            goal = jnp.where(plane == source, target, goal)
        return goal

    keep_a = right_place & (src_plane == sent_to(ROUND_A))
    crossing = (plane == CROSSING[0]) | (plane == CROSSING[1])
    keep_b = right_place & (src_plane == sent_to(ROUND_B))
    keep_b = keep_b & (src_core == jnp.where(crossing, 1 - core, core))
    sums = jnp.where(keep_row, picked[:, :samples], 0.0)
    sums = sums + jnp.where(keep_a, picked[:, samples : 2 * samples], 0.0)
    sums = sums + jnp.where(keep_b, picked[:, 2 * samples :], 0.0)
    proof_ref[...] = jnp.sum(sums, axis=0, keepdims=True) * factor
    row = lax.broadcasted_iota(jnp.int32, (samples, LANES), 0)
    lane = lax.broadcasted_iota(jnp.int32, (samples, LANES), 1)
    is_total = (lane == places + 4) & (int_mod(row, per_peer) == 0)
    total = jnp.sum(jnp.where(is_total, got, 0.0), axis=(0, 1), keepdims=True)
    mmd_ref[...] = total * factor * (1.0 / half_count)


def in_vmem(array):
    return pltpu.with_memory_space_constraint(array, pltpu.VMEM)


def in_hbm(array):
    return pltpu.with_memory_space_constraint(array, pltpu.HBM)


def vmem_specs(count):
    return [pl.BlockSpec(memory_space=pltpu.VMEM)] * count


def local(embeddings, labels, source_id):
    layout = Layout(lax.axis_size("row"), lax.axis_size("col"))
    places = layout.places
    samples, width = embeddings.shape
    chunks = width // LANES
    per_peer = samples // layout.devices
    half_count = samples * layout.devices // 2
    factor = 1000.0 / half_count
    tiles = -(-samples // LANES)
    pack_rows = samples * chunks + tiles * SUBLANES
    key_rows = (CORES + FAR_BLOCKS) * samples
    query_rows = places * samples
    block_bytes = pack_rows * LANES * 4
    work_bytes = (key_rows + query_rows) * width * 6 + 8 * GROUP_ROWS * key_rows * 4
    params = pltpu.CompilerParams(vmem_limit_bytes=work_bytes + 4 * MIB)

    packed, ids = pl.pallas_call(
        pack_kernel,
        out_shape=(
            pltpu.VMEM((pack_rows, LANES), jnp.float32),
            pltpu.VMEM((1, samples), jnp.int32),
        ),
        in_specs=vmem_specs(3),
        out_specs=tuple(vmem_specs(2)),
        compiler_params=pltpu.CompilerParams(vmem_limit_bytes=4 * block_bytes + 4 * MIB),
        name="pack_block",
    )(
        in_hbm(embeddings),
        in_hbm(labels.reshape(1, samples)),
        in_hbm(source_id.reshape(1, samples)),
    )

    def send(block, target):
        return lax.ppermute(block, ("row", "col"), layout.pairs(target))

    def round_a(plane, place, core):
        return (ROUND_A[plane], place, core)

    def round_b(plane, place, core):
        return (ROUND_B[plane], place, 1 - core if plane in CROSSING else core)

    def to_place(step):
        return lambda plane, place, core: (plane, place ^ step, core)

    def to_core(plane, place, core):
        return (plane, place, 1 - core)

    far_b = send(packed, round_b)
    in_plane = [None] + [send(packed, to_place(step)) for step in range(1, places)]
    far_a = send(packed, round_a)
    late_a, *_ = lax.optimization_barrier((far_a, in_plane[2], in_plane[1]))
    far_a_other = send(late_a, to_core)
    late, *_ = lax.optimization_barrier((packed, in_plane[2]))
    near = send(late, to_core)

    blocks = [packed, *in_plane[1:], near, far_a, far_a_other, far_b]
    partial = pl.pallas_call(
        functools.partial(main_kernel, samples, chunks, layout),
        out_shape=pltpu.VMEM((samples, LANES), jnp.float32),
        in_specs=vmem_specs(len(blocks)),
        out_specs=pl.BlockSpec(memory_space=pltpu.VMEM),
        scratch_shapes=[
            pltpu.VMEM((2 * key_rows, width), jnp.bfloat16),
            pltpu.VMEM((2 * query_rows, width), jnp.bfloat16),
            pltpu.VMEM((SUBLANES, query_rows), jnp.float32),
        ],
        compiler_params=params,
        name="kernel_sums",
    )(*[in_vmem(block) for block in blocks])

    got = lax.all_to_all(partial, ("row", "col"), split_axis=0, concat_axis=0, tiled=True)

    proof, mmd = pl.pallas_call(
        functools.partial(last_kernel, layout, samples, per_peer, factor, half_count),
        out_shape=(
            jax.ShapeDtypeStruct((1, samples), jnp.float32),
            jax.ShapeDtypeStruct((1, 1), jnp.float32),
        ),
        in_specs=vmem_specs(2),
        out_specs=tuple(vmem_specs(2)),
        compiler_params=pltpu.CompilerParams(vmem_limit_bytes=16 * MIB),
        name="pick_proof",
    )(in_vmem(got), in_vmem(ids))
    return proof.reshape(samples), mmd.reshape(())


def solution(mesh):
    return jax.shard_map(
        local,
        mesh=mesh,
        in_specs=(P(("row", "col"), None), P(("row", "col")), P(("row", "col"))),
        out_specs=(P(("row", "col")), P()),
        check_vma=False,
    )
```

```python
import functools

import jax
import jax.numpy as jnp
from jax import lax
from jax.experimental import pallas as pl
from jax.experimental.pallas import tpu as pltpu
from jax.sharding import PartitionSpec as P

LANES = 128
SUBLANES = 8
GROUP_ROWS = 256
PLANES = 4
CORES = 2
ROUND_A = {2: 0, 3: 1, 1: 2, 0: 3}
ROUND_B = {0: 1, 3: 2, 1: 0, 2: 3}
CROSSING = (1, 2)
FAR_BLOCKS = 3
MIB = 1024 * 1024
NT_DIMS = (((1,), (1,)), ((), ()))
NN_DIMS = (((1,), (0,)), ((), ()))


def int_div(value, divisor):
    if divisor & (divisor - 1) == 0:
        return lax.shift_right_logical(value, divisor.bit_length() - 1)
    return value // divisor


def int_mod(value, divisor):
    if divisor & (divisor - 1) == 0:
        return value & (divisor - 1)
    return value % divisor


class Layout:
    def __init__(self, row_count, col_count):
        self.core_in_row = row_count == PLANES * CORES
        self.places = col_count if self.core_in_row else col_count // CORES
        self.devices = row_count * col_count

    def flat(self, plane, place, core):
        if self.core_in_row:
            return (plane * CORES + core) * self.places + place
        return (plane * self.places + place) * CORES + core

    def parts(self, flat):
        if self.core_in_row:
            place, rest = int_mod(flat, self.places), int_div(flat, self.places)
            return int_div(rest, CORES), place, int_mod(rest, CORES)
        core, rest = int_mod(flat, CORES), int_div(flat, CORES)
        return int_div(rest, self.places), int_mod(rest, self.places), core

    def here(self):
        row, col = lax.axis_index("row"), lax.axis_index("col")
        if self.core_in_row:
            return int_div(row, CORES), col, int_mod(row, CORES)
        return row, int_div(col, CORES), int_mod(col, CORES)

    def pairs(self, target):
        result = []
        for plane in range(PLANES):
            for place in range(self.places):
                for core in range(CORES):
                    goal = target(plane, place, core)
                    result.append((self.flat(plane, place, core), self.flat(*goal)))
        return sorted(result)


def split2(value):
    high = value.astype(jnp.bfloat16)
    return high, (value - high.astype(jnp.float32)).astype(jnp.bfloat16)


def split3(value):
    high = value.astype(jnp.bfloat16)
    rest = value - high.astype(jnp.float32)
    mid = rest.astype(jnp.bfloat16)
    low = (rest - mid.astype(jnp.float32)).astype(jnp.bfloat16)
    return high, mid, low


def bf16_dot(left, right, dims):
    return lax.dot_general(left, right, dims, preferred_element_type=jnp.float32)


def pack_kernel(emb_ref, label_ref, id_ref, out_ref, id_out_ref, label_vmem, copied):
    samples, width = emb_ref.shape
    chunks = width // LANES
    copies = [
        pltpu.make_async_copy(
            emb_ref.at[:, pl.ds(chunk * LANES, LANES)],
            out_ref.at[pl.ds(chunk * samples, samples), :],
            copied.at[chunk],
        )
        for chunk in range(chunks)
    ]
    copies.append(pltpu.make_async_copy(label_ref, label_vmem, copied.at[chunks]))
    copies.append(pltpu.make_async_copy(id_ref, id_out_ref, copied.at[chunks + 1]))
    for copy in copies:
        copy.start()
    squares = jnp.zeros((samples, LANES), jnp.float32)
    for chunk in range(chunks):
        copies[chunk].wait()
        value = out_ref[pl.ds(chunk * samples, samples), :]
        squares = squares + value * value
    ones = jnp.ones((SUBLANES, LANES), jnp.bfloat16)
    high, mid, low = (bf16_dot(ones, part, NT_DIMS) for part in split3(squares))
    norm = high + (mid + low)
    copies[chunks].wait()
    sign = (1 - 2 * label_vmem[...]).astype(jnp.float32)
    base = samples * chunks
    row = lax.broadcasted_iota(jnp.int32, (SUBLANES, samples), 0)
    both = jnp.where(row == 0, sign, norm)
    for start in range(0, samples, LANES):
        lanes = min(LANES, samples - start)
        place = base + start // LANES * SUBLANES
        if lanes < LANES:
            out_ref[pl.ds(place, SUBLANES), :] = jnp.zeros((SUBLANES, LANES), jnp.float32)
        out_ref[pl.ds(place, SUBLANES), pl.ds(0, lanes)] = both[:, start : start + lanes]
    copies[chunks + 1].wait()


def stage(ref, scratch, start, middle, samples, chunks):
    for chunk in range(chunks):
        value = ref[pl.ds(chunk * samples, samples), :]
        for offset, piece in zip((0, middle), split2(value)):
            scratch[pl.ds(offset + start, samples), pl.ds(chunk * LANES, LANES)] = piece


def tail_rows(refs, samples, chunks):
    pieces = []
    for ref in refs:
        for start in range(0, samples, LANES):
            lanes = min(LANES, samples - start)
            place = samples * chunks + start // LANES * SUBLANES
            pieces.append(ref[pl.ds(place, SUBLANES), pl.ds(0, lanes)])
    return jnp.concatenate(pieces, axis=1)


def as_columns(rows):
    count = rows.shape[1]
    fill = -count % LANES
    if fill:
        rows = jnp.concatenate([rows, jnp.zeros((SUBLANES, fill), jnp.float32)], axis=1)
    return jnp.transpose(rows)[:count]


def main_kernel(samples, chunks, layout, *refs):
    places = layout.places
    queries = refs[:places]
    keys = (refs[0],) + refs[places : places + 4]
    out_ref, key_parts, query_parts, tail_ref = refs[places + 4 :]
    _, me_place, me_core = layout.here()
    rows = places * samples
    key_rows = len(keys) * samples
    group = min(GROUP_ROWS, rows)
    blocks = group // samples
    near = CORES * samples
    for place, ref in enumerate(queries):
        stage(ref, query_parts, place * samples, rows, samples, chunks)
    for place, ref in enumerate(keys):
        stage(ref, key_parts, place * samples, key_rows, samples, chunks)
    key_tail = as_columns(tail_rows(keys, samples, chunks))
    key_sign, key_norm = key_tail[:, 0:1], key_tail[:, 1:2]
    tail_ref[...] = tail_rows(queries, samples, chunks)
    lane = lax.broadcasted_iota(jnp.int32, (samples, LANES), 1)

    def one_group(index, carry):
        result, total, column = carry
        start = pl.multiple_of(index * group, group)
        both = key_parts[...]
        by_high = bf16_dot(both, query_parts[pl.ds(start, group), :], NT_DIMS)
        by_mid = bf16_dot(both, query_parts[pl.ds(rows + start, group), :], NT_DIMS)
        inner = by_high[:key_rows] + (by_high[key_rows:] + by_mid[:key_rows] + by_mid[key_rows:])
        sign = tail_ref[0:1, pl.ds(start, group)]
        norm = tail_ref[1:2, pl.ds(start, group)]
        sq_dist = norm + key_norm - 2.0 * inner
        kernel = jnp.exp(sq_dist * (-1.0 / 200.0))
        signed = kernel * key_sign
        near_sums = jnp.sum(signed[:near], axis=0, keepdims=True)
        far_sums = jnp.sum(signed[near:], axis=0, keepdims=True)
        sums = near_sums + far_sums
        total = total + jnp.sum(sign * (sums + far_sums), axis=1, keepdims=True)
        column = column + jnp.sum(kernel[near:] * sign, axis=1, keepdims=True)
        sums = as_columns(jnp.broadcast_to(sums, (SUBLANES, group)))
        for place in range(blocks):
            owner = me_place ^ (index * blocks + place)
            result = jnp.where(
                lane == owner, sums[place * samples : (place + 1) * samples, 0:1], result
            )
        return result, total, column

    carry = (
        jnp.zeros((samples, LANES), jnp.float32),
        jnp.zeros((1, 1), jnp.float32),
        jnp.zeros((FAR_BLOCKS * samples, 1), jnp.float32),
    )
    if rows == group:
        carry = one_group(0, carry)
    else:
        carry = lax.fori_loop(0, rows // group, one_group, carry)
    result, total, column = carry
    for place, offset in enumerate((me_core, 1 - me_core, 2)):
        result = jnp.where(
            lane == places + offset, column[place * samples : (place + 1) * samples], result
        )
    out_ref[...] = jnp.where(lane == places + 4, total, result)


def last_kernel(layout, samples, per_peer, factor, half_count, got_ref, id_ref, proof_ref, mmd_ref):
    got = got_ref[...]
    ids = id_ref[...]
    places = layout.places
    plane, place, core = layout.parts(int_div(ids, samples))
    slot = int_mod(ids, per_peer)
    targets = jnp.concatenate(
        [place, places + core, jnp.full(core.shape, places + 2, jnp.int32)], axis=1
    )
    lane_of = lax.broadcasted_iota(jnp.int32, (LANES, 3 * samples), 0)
    picks = jnp.where(lane_of == targets, 1.0, 0.0).astype(jnp.bfloat16)
    high, mid, low = split3(got)
    picked = bf16_dot(high, picks, NN_DIMS) + (
        bf16_dot(mid, picks, NN_DIMS) + bf16_dot(low, picks, NN_DIMS)
    )
    row = lax.broadcasted_iota(jnp.int32, (samples, samples), 0)
    src_plane, src_place, src_core = layout.parts(int_div(row, per_peer))
    right_slot = int_mod(row, per_peer) == slot
    keep_row = right_slot & (src_plane == plane) & (src_core == core)
    right_place = right_slot & (src_place == place)

    def sent_to(table):
        goal = jnp.full(plane.shape, -1, jnp.int32)
        for source, target in table.items():
            goal = jnp.where(plane == source, target, goal)
        return goal

    keep_a = right_place & (src_plane == sent_to(ROUND_A))
    crossing = (plane == CROSSING[0]) | (plane == CROSSING[1])
    keep_b = right_place & (src_plane == sent_to(ROUND_B))
    keep_b = keep_b & (src_core == jnp.where(crossing, 1 - core, core))
    sums = jnp.where(keep_row, picked[:, :samples], 0.0)
    sums = sums + jnp.where(keep_a, picked[:, samples : 2 * samples], 0.0)
    sums = sums + jnp.where(keep_b, picked[:, 2 * samples :], 0.0)
    proof_ref[...] = jnp.sum(sums, axis=0, keepdims=True) * factor
    row = lax.broadcasted_iota(jnp.int32, (samples, LANES), 0)
    lane = lax.broadcasted_iota(jnp.int32, (samples, LANES), 1)
    is_total = (lane == places + 4) & (int_mod(row, per_peer) == 0)
    total = jnp.sum(jnp.where(is_total, got, 0.0), axis=(0, 1), keepdims=True)
    mmd_ref[...] = total * factor * (1.0 / half_count)


def in_vmem(array):
    return pltpu.with_memory_space_constraint(array, pltpu.VMEM)


def in_hbm(array):
    return pltpu.with_memory_space_constraint(array, pltpu.HBM)


def vmem_specs(count):
    return [pl.BlockSpec(memory_space=pltpu.VMEM)] * count


def local(embeddings, labels, source_id):
    layout = Layout(lax.axis_size("row"), lax.axis_size("col"))
    places = layout.places
    samples, width = embeddings.shape
    chunks = width // LANES
    per_peer = samples // layout.devices
    half_count = samples * layout.devices // 2
    factor = 1000.0 / half_count
    tiles = -(-samples // LANES)
    pack_rows = samples * chunks + tiles * SUBLANES
    key_rows = (CORES + FAR_BLOCKS) * samples
    query_rows = places * samples
    block_bytes = pack_rows * LANES * 4
    work_bytes = (key_rows + query_rows) * width * 6 + 8 * GROUP_ROWS * key_rows * 4
    params = pltpu.CompilerParams(vmem_limit_bytes=work_bytes + 4 * MIB)

    packed, ids = pl.pallas_call(
        pack_kernel,
        out_shape=(
            pltpu.VMEM((pack_rows, LANES), jnp.float32),
            pltpu.VMEM((1, samples), jnp.int32),
        ),
        in_specs=[pl.BlockSpec(memory_space=pl.ANY)] * 3,
        out_specs=tuple(vmem_specs(2)),
        scratch_shapes=[
            pltpu.VMEM((1, samples), jnp.int32),
            pltpu.SemaphoreType.DMA((chunks + 2,)),
        ],
        compiler_params=pltpu.CompilerParams(vmem_limit_bytes=4 * block_bytes + 4 * MIB),
        name="pack_block",
    )(
        in_hbm(embeddings),
        in_hbm(labels.reshape(1, samples)),
        in_hbm(source_id.reshape(1, samples)),
    )

    def send(block, target):
        return lax.ppermute(block, ("row", "col"), layout.pairs(target))

    def round_a(plane, place, core):
        return (ROUND_A[plane], place, core)

    def round_b(plane, place, core):
        return (ROUND_B[plane], place, 1 - core if plane in CROSSING else core)

    def to_place(step):
        return lambda plane, place, core: (plane, place ^ step, core)

    def to_core(plane, place, core):
        return (plane, place, 1 - core)

    in_plane = [send(packed, to_place(step)) for step in range(1, places)]
    far_b = send(packed, round_b)
    far_a = send(packed, round_a)
    far_a_other = send(far_a, to_core)
    late, *_ = lax.optimization_barrier((packed, in_plane[-1], far_a))
    near = send(late, to_core)

    blocks = [packed, *in_plane, near, far_a, far_a_other, far_b]
    partial = pl.pallas_call(
        functools.partial(main_kernel, samples, chunks, layout),
        out_shape=pltpu.VMEM((samples, LANES), jnp.float32),
        in_specs=vmem_specs(len(blocks)),
        out_specs=pl.BlockSpec(memory_space=pltpu.VMEM),
        scratch_shapes=[
            pltpu.VMEM((2 * key_rows, width), jnp.bfloat16),
            pltpu.VMEM((2 * query_rows, width), jnp.bfloat16),
            pltpu.VMEM((SUBLANES, query_rows), jnp.float32),
        ],
        compiler_params=params,
        name="kernel_sums",
    )(*[in_vmem(block) for block in blocks])

    got = lax.all_to_all(partial, ("row", "col"), split_axis=0, concat_axis=0, tiled=True)

    proof, mmd = pl.pallas_call(
        functools.partial(last_kernel, layout, samples, per_peer, factor, half_count),
        out_shape=(
            jax.ShapeDtypeStruct((1, samples), jnp.float32),
            jax.ShapeDtypeStruct((1, 1), jnp.float32),
        ),
        in_specs=vmem_specs(2),
        out_specs=tuple(vmem_specs(2)),
        compiler_params=pltpu.CompilerParams(vmem_limit_bytes=16 * MIB),
        name="pick_proof",
    )(in_vmem(got), in_vmem(ids))
    return proof.reshape(samples), mmd.reshape(())


def solution(mesh):
    return jax.shard_map(
        local,
        mesh=mesh,
        in_specs=(P(("row", "col"), None), P(("row", "col")), P(("row", "col"))),
        out_specs=(P(("row", "col")), P()),
        check_vma=False,
    )
```

```python
import functools

import jax
import jax.numpy as jnp
from jax import lax
from jax.experimental import pallas as pl
from jax.experimental.pallas import tpu as pltpu
from jax.sharding import PartitionSpec as P

LANES = 128
SUBLANES = 8
GROUP_ROWS = 256
PLANES = 4
CORES = 2
ROUND_A = {2: 0, 3: 1, 1: 2, 0: 3}
ROUND_B = {0: 1, 3: 2, 1: 0, 2: 3}
CROSSING = (0, 3)
FAR_BLOCKS = 3
MIB = 1024 * 1024
NT_DIMS = (((1,), (1,)), ((), ()))
NN_DIMS = (((1,), (0,)), ((), ()))


def int_div(value, divisor):
    if divisor & (divisor - 1) == 0:
        return lax.shift_right_logical(value, divisor.bit_length() - 1)
    return value // divisor


def int_mod(value, divisor):
    if divisor & (divisor - 1) == 0:
        return value & (divisor - 1)
    return value % divisor


class Layout:
    def __init__(self, row_count, col_count):
        self.core_in_row = row_count == PLANES * CORES
        self.places = col_count if self.core_in_row else col_count // CORES
        self.devices = row_count * col_count

    def flat(self, plane, place, core):
        if self.core_in_row:
            return (plane * CORES + core) * self.places + place
        return (plane * self.places + place) * CORES + core

    def parts(self, flat):
        if self.core_in_row:
            place, rest = int_mod(flat, self.places), int_div(flat, self.places)
            return int_div(rest, CORES), place, int_mod(rest, CORES)
        core, rest = int_mod(flat, CORES), int_div(flat, CORES)
        return int_div(rest, self.places), int_mod(rest, self.places), core

    def here(self):
        row, col = lax.axis_index("row"), lax.axis_index("col")
        if self.core_in_row:
            return int_div(row, CORES), col, int_mod(row, CORES)
        return row, int_div(col, CORES), int_mod(col, CORES)

    def pairs(self, target):
        result = []
        for plane in range(PLANES):
            for place in range(self.places):
                for core in range(CORES):
                    goal = target(plane, place, core)
                    result.append((self.flat(plane, place, core), self.flat(*goal)))
        return sorted(result)


def split2(value):
    high = value.astype(jnp.bfloat16)
    return high, (value - high.astype(jnp.float32)).astype(jnp.bfloat16)


def split3(value):
    high = value.astype(jnp.bfloat16)
    rest = value - high.astype(jnp.float32)
    mid = rest.astype(jnp.bfloat16)
    low = (rest - mid.astype(jnp.float32)).astype(jnp.bfloat16)
    return high, mid, low


def bf16_dot(left, right, dims):
    return lax.dot_general(left, right, dims, preferred_element_type=jnp.float32)


def pack_kernel(emb_ref, label_ref, id_ref, out_ref, id_out_ref, label_vmem, copied):
    samples, width = emb_ref.shape
    chunks = width // LANES
    copies = [
        pltpu.make_async_copy(
            emb_ref.at[:, pl.ds(chunk * LANES, LANES)],
            out_ref.at[pl.ds(chunk * samples, samples), :],
            copied.at[chunk],
        )
        for chunk in range(chunks)
    ]
    copies.append(pltpu.make_async_copy(label_ref, label_vmem, copied.at[chunks]))
    copies.append(pltpu.make_async_copy(id_ref, id_out_ref, copied.at[chunks + 1]))
    for copy in copies:
        copy.start()
    squares = jnp.zeros((samples, LANES), jnp.float32)
    for chunk in range(chunks):
        copies[chunk].wait()
        value = out_ref[pl.ds(chunk * samples, samples), :]
        squares = squares + value * value
    ones = jnp.ones((SUBLANES, LANES), jnp.bfloat16)
    high, mid, low = (bf16_dot(ones, part, NT_DIMS) for part in split3(squares))
    norm = high + (mid + low)
    copies[chunks].wait()
    sign = (1 - 2 * label_vmem[...]).astype(jnp.float32)
    base = samples * chunks
    row = lax.broadcasted_iota(jnp.int32, (SUBLANES, samples), 0)
    both = jnp.where(row == 0, sign, norm)
    for start in range(0, samples, LANES):
        lanes = min(LANES, samples - start)
        place = base + start // LANES * SUBLANES
        if lanes < LANES:
            out_ref[pl.ds(place, SUBLANES), :] = jnp.zeros((SUBLANES, LANES), jnp.float32)
        out_ref[pl.ds(place, SUBLANES), pl.ds(0, lanes)] = both[:, start : start + lanes]
    copies[chunks + 1].wait()


def stage(ref, scratch, start, middle, samples, chunks):
    for chunk in range(chunks):
        value = ref[pl.ds(chunk * samples, samples), :]
        for offset, piece in zip((0, middle), split2(value)):
            scratch[pl.ds(offset + start, samples), pl.ds(chunk * LANES, LANES)] = piece


def tail_rows(refs, samples, chunks):
    pieces = []
    for ref in refs:
        for start in range(0, samples, LANES):
            lanes = min(LANES, samples - start)
            place = samples * chunks + start // LANES * SUBLANES
            pieces.append(ref[pl.ds(place, SUBLANES), pl.ds(0, lanes)])
    return jnp.concatenate(pieces, axis=1)


def as_columns(rows):
    count = rows.shape[1]
    fill = -count % LANES
    if fill:
        rows = jnp.concatenate([rows, jnp.zeros((SUBLANES, fill), jnp.float32)], axis=1)
    return jnp.transpose(rows)[:count]


def main_kernel(samples, chunks, layout, *refs):
    places = layout.places
    queries = refs[:places]
    keys = (refs[0],) + refs[places : places + 4]
    out_ref, key_parts, query_parts, tail_ref = refs[places + 4 :]
    _, me_place, me_core = layout.here()
    rows = places * samples
    key_rows = len(keys) * samples
    group = min(GROUP_ROWS, rows)
    blocks = group // samples
    near = CORES * samples
    for place, ref in enumerate(queries):
        stage(ref, query_parts, place * samples, rows, samples, chunks)
    for place, ref in enumerate(keys):
        stage(ref, key_parts, place * samples, key_rows, samples, chunks)
    key_tail = as_columns(tail_rows(keys, samples, chunks))
    key_sign, key_norm = key_tail[:, 0:1], key_tail[:, 1:2]
    tail_ref[...] = tail_rows(queries, samples, chunks)
    lane = lax.broadcasted_iota(jnp.int32, (samples, LANES), 1)

    def one_group(index, carry):
        result, total, column = carry
        start = pl.multiple_of(index * group, group)
        both = key_parts[...]
        by_high = bf16_dot(both, query_parts[pl.ds(start, group), :], NT_DIMS)
        by_mid = bf16_dot(both, query_parts[pl.ds(rows + start, group), :], NT_DIMS)
        inner = by_high[:key_rows] + (by_high[key_rows:] + by_mid[:key_rows] + by_mid[key_rows:])
        sign = tail_ref[0:1, pl.ds(start, group)]
        norm = tail_ref[1:2, pl.ds(start, group)]
        sq_dist = norm + key_norm - 2.0 * inner
        kernel = jnp.exp(sq_dist * (-1.0 / 200.0))
        signed = kernel * key_sign
        near_sums = jnp.sum(signed[:near], axis=0, keepdims=True)
        far_sums = jnp.sum(signed[near:], axis=0, keepdims=True)
        sums = near_sums + far_sums
        total = total + jnp.sum(sign * (sums + far_sums), axis=1, keepdims=True)
        column = column + jnp.sum(kernel[near:] * sign, axis=1, keepdims=True)
        sums = as_columns(jnp.broadcast_to(sums, (SUBLANES, group)))
        for place in range(blocks):
            owner = me_place ^ (index * blocks + place)
            result = jnp.where(
                lane == owner, sums[place * samples : (place + 1) * samples, 0:1], result
            )
        return result, total, column

    carry = (
        jnp.zeros((samples, LANES), jnp.float32),
        jnp.zeros((1, 1), jnp.float32),
        jnp.zeros((FAR_BLOCKS * samples, 1), jnp.float32),
    )
    if rows == group:
        carry = one_group(0, carry)
    else:
        carry = lax.fori_loop(0, rows // group, one_group, carry)
    result, total, column = carry
    for place, offset in enumerate((me_core, 1 - me_core, 2)):
        result = jnp.where(
            lane == places + offset, column[place * samples : (place + 1) * samples], result
        )
    out_ref[...] = jnp.where(lane == places + 4, total, result)


def last_kernel(layout, samples, per_peer, factor, half_count, got_ref, id_ref, proof_ref, mmd_ref):
    got = got_ref[...]
    ids = id_ref[...]
    places = layout.places
    plane, place, core = layout.parts(int_div(ids, samples))
    slot = int_mod(ids, per_peer)
    targets = jnp.concatenate(
        [place, places + core, jnp.full(core.shape, places + 2, jnp.int32)], axis=1
    )
    lane_of = lax.broadcasted_iota(jnp.int32, (LANES, 3 * samples), 0)
    picks = jnp.where(lane_of == targets, 1.0, 0.0).astype(jnp.bfloat16)
    high, mid, low = split3(got)
    picked = bf16_dot(high, picks, NN_DIMS) + (
        bf16_dot(mid, picks, NN_DIMS) + bf16_dot(low, picks, NN_DIMS)
    )
    row = lax.broadcasted_iota(jnp.int32, (samples, samples), 0)
    src_plane, src_place, src_core = layout.parts(int_div(row, per_peer))
    right_slot = int_mod(row, per_peer) == slot
    keep_row = right_slot & (src_plane == plane) & (src_core == core)
    right_place = right_slot & (src_place == place)

    def sent_to(table):
        goal = jnp.full(plane.shape, -1, jnp.int32)
        for source, target in table.items():
            goal = jnp.where(plane == source, target, goal)
        return goal

    keep_a = right_place & (src_plane == sent_to(ROUND_A))
    crossing = (plane == CROSSING[0]) | (plane == CROSSING[1])
    keep_b = right_place & (src_plane == sent_to(ROUND_B))
    keep_b = keep_b & (src_core == jnp.where(crossing, 1 - core, core))
    sums = jnp.where(keep_row, picked[:, :samples], 0.0)
    sums = sums + jnp.where(keep_a, picked[:, samples : 2 * samples], 0.0)
    sums = sums + jnp.where(keep_b, picked[:, 2 * samples :], 0.0)
    proof_ref[...] = jnp.sum(sums, axis=0, keepdims=True) * factor
    row = lax.broadcasted_iota(jnp.int32, (samples, LANES), 0)
    lane = lax.broadcasted_iota(jnp.int32, (samples, LANES), 1)
    is_total = (lane == places + 4) & (int_mod(row, per_peer) == 0)
    total = jnp.sum(jnp.where(is_total, got, 0.0), axis=(0, 1), keepdims=True)
    mmd_ref[...] = total * factor * (1.0 / half_count)


def in_vmem(array):
    return pltpu.with_memory_space_constraint(array, pltpu.VMEM)


def in_hbm(array):
    return pltpu.with_memory_space_constraint(array, pltpu.HBM)


def vmem_specs(count):
    return [pl.BlockSpec(memory_space=pltpu.VMEM)] * count


def local(embeddings, labels, source_id):
    layout = Layout(lax.axis_size("row"), lax.axis_size("col"))
    places = layout.places
    samples, width = embeddings.shape
    chunks = width // LANES
    per_peer = samples // layout.devices
    half_count = samples * layout.devices // 2
    factor = 1000.0 / half_count
    tiles = -(-samples // LANES)
    pack_rows = samples * chunks + tiles * SUBLANES
    key_rows = (CORES + FAR_BLOCKS) * samples
    query_rows = places * samples
    block_bytes = pack_rows * LANES * 4
    work_bytes = (key_rows + query_rows) * width * 6 + 8 * GROUP_ROWS * key_rows * 4
    params = pltpu.CompilerParams(vmem_limit_bytes=work_bytes + 4 * MIB)

    packed, ids = pl.pallas_call(
        pack_kernel,
        out_shape=(
            pltpu.VMEM((pack_rows, LANES), jnp.float32),
            pltpu.VMEM((1, samples), jnp.int32),
        ),
        in_specs=[pl.BlockSpec(memory_space=pl.ANY)] * 3,
        out_specs=tuple(vmem_specs(2)),
        scratch_shapes=[
            pltpu.VMEM((1, samples), jnp.int32),
            pltpu.SemaphoreType.DMA((chunks + 2,)),
        ],
        compiler_params=pltpu.CompilerParams(vmem_limit_bytes=4 * block_bytes + 4 * MIB),
        name="pack_block",
    )(
        in_hbm(embeddings),
        in_hbm(labels.reshape(1, samples)),
        in_hbm(source_id.reshape(1, samples)),
    )

    def send(block, target):
        return lax.ppermute(block, ("row", "col"), layout.pairs(target))

    def round_a(plane, place, core):
        return (ROUND_A[plane], place, core)

    def round_b(plane, place, core):
        return (ROUND_B[plane], place, 1 - core if plane in CROSSING else core)

    def to_place(step):
        return lambda plane, place, core: (plane, place ^ step, core)

    def to_core(plane, place, core):
        return (plane, place, 1 - core)

    in_plane = [send(packed, to_place(step)) for step in range(1, places)]
    far_b = send(packed, round_b)
    far_a = send(packed, round_a)
    far_a_other = send(far_a, to_core)
    late, *_ = lax.optimization_barrier((packed, in_plane[-1], far_a))
    near = send(late, to_core)

    blocks = [packed, *in_plane, near, far_a, far_a_other, far_b]
    partial = pl.pallas_call(
        functools.partial(main_kernel, samples, chunks, layout),
        out_shape=pltpu.VMEM((samples, LANES), jnp.float32),
        in_specs=vmem_specs(len(blocks)),
        out_specs=pl.BlockSpec(memory_space=pltpu.VMEM),
        scratch_shapes=[
            pltpu.VMEM((2 * key_rows, width), jnp.bfloat16),
            pltpu.VMEM((2 * query_rows, width), jnp.bfloat16),
            pltpu.VMEM((SUBLANES, query_rows), jnp.float32),
        ],
        compiler_params=params,
        name="kernel_sums",
    )(*[in_vmem(block) for block in blocks])

    got = lax.all_to_all(partial, ("row", "col"), split_axis=0, concat_axis=0, tiled=True)

    proof, mmd = pl.pallas_call(
        functools.partial(last_kernel, layout, samples, per_peer, factor, half_count),
        out_shape=(
            jax.ShapeDtypeStruct((1, samples), jnp.float32),
            jax.ShapeDtypeStruct((1, 1), jnp.float32),
        ),
        in_specs=vmem_specs(2),
        out_specs=tuple(vmem_specs(2)),
        compiler_params=pltpu.CompilerParams(vmem_limit_bytes=16 * MIB),
        name="pick_proof",
    )(in_vmem(got), in_vmem(ids))
    return proof.reshape(samples), mmd.reshape(())


def solution(mesh):
    return jax.shard_map(
        local,
        mesh=mesh,
        in_specs=(P(("row", "col"), None), P(("row", "col")), P(("row", "col"))),
        out_specs=(P(("row", "col")), P()),
        check_vma=False,
    )
```

```python
import functools

import jax
import jax.numpy as jnp
from jax import lax
from jax.experimental import pallas as pl
from jax.experimental.pallas import tpu as pltpu
from jax.sharding import PartitionSpec as P

LANES = 128
SUBLANES = 8
GROUP_ROWS = 256
PLANES = 4
CORES = 2
ROUND_A = {2: 0, 3: 1, 1: 2, 0: 3}
ROUND_B = {0: 1, 3: 2, 1: 0, 2: 3}
CROSSING = (0, 3)
FAR_BLOCKS = 3
MIB = 1024 * 1024
NT_DIMS = (((1,), (1,)), ((), ()))
NN_DIMS = (((1,), (0,)), ((), ()))


def int_div(value, divisor):
    if divisor & (divisor - 1) == 0:
        return lax.shift_right_logical(value, divisor.bit_length() - 1)
    return value // divisor


def int_mod(value, divisor):
    if divisor & (divisor - 1) == 0:
        return value & (divisor - 1)
    return value % divisor


class Layout:
    def __init__(self, row_count, col_count):
        self.core_in_row = row_count == PLANES * CORES
        self.places = col_count if self.core_in_row else col_count // CORES
        self.devices = row_count * col_count

    def flat(self, plane, place, core):
        if self.core_in_row:
            return (plane * CORES + core) * self.places + place
        return (plane * self.places + place) * CORES + core

    def parts(self, flat):
        if self.core_in_row:
            place, rest = int_mod(flat, self.places), int_div(flat, self.places)
            return int_div(rest, CORES), place, int_mod(rest, CORES)
        core, rest = int_mod(flat, CORES), int_div(flat, CORES)
        return int_div(rest, self.places), int_mod(rest, self.places), core

    def here(self):
        row, col = lax.axis_index("row"), lax.axis_index("col")
        if self.core_in_row:
            return int_div(row, CORES), col, int_mod(row, CORES)
        return row, int_div(col, CORES), int_mod(col, CORES)

    def pairs(self, target):
        result = []
        for plane in range(PLANES):
            for place in range(self.places):
                for core in range(CORES):
                    goal = target(plane, place, core)
                    result.append((self.flat(plane, place, core), self.flat(*goal)))
        return sorted(result)


def split2(value):
    high = value.astype(jnp.bfloat16)
    return high, (value - high.astype(jnp.float32)).astype(jnp.bfloat16)


def split3(value):
    high = value.astype(jnp.bfloat16)
    rest = value - high.astype(jnp.float32)
    mid = rest.astype(jnp.bfloat16)
    low = (rest - mid.astype(jnp.float32)).astype(jnp.bfloat16)
    return high, mid, low


def bf16_dot(left, right, dims):
    return lax.dot_general(left, right, dims, preferred_element_type=jnp.float32)


def pack_kernel(emb_ref, label_ref, id_ref, out_ref, id_out_ref, label_vmem, copied):
    samples, width = emb_ref.shape
    chunks = width // LANES
    copies = [
        pltpu.make_async_copy(
            emb_ref.at[:, pl.ds(chunk * LANES, LANES)],
            out_ref.at[pl.ds(chunk * samples, samples), :],
            copied.at[chunk],
        )
        for chunk in range(chunks)
    ]
    copies.append(pltpu.make_async_copy(label_ref, label_vmem, copied.at[chunks]))
    copies.append(pltpu.make_async_copy(id_ref, id_out_ref, copied.at[chunks + 1]))
    for copy in copies:
        copy.start()
    squares = jnp.zeros((samples, LANES), jnp.float32)
    for chunk in range(chunks):
        copies[chunk].wait()
        value = out_ref[pl.ds(chunk * samples, samples), :]
        squares = squares + value * value
    ones = jnp.ones((SUBLANES, LANES), jnp.bfloat16)
    high, mid, low = (bf16_dot(ones, part, NT_DIMS) for part in split3(squares))
    norm = high + (mid + low)
    copies[chunks].wait()
    sign = (1 - 2 * label_vmem[...]).astype(jnp.float32)
    base = samples * chunks
    row = lax.broadcasted_iota(jnp.int32, (SUBLANES, samples), 0)
    both = jnp.where(row == 0, sign, norm)
    for start in range(0, samples, LANES):
        lanes = min(LANES, samples - start)
        place = base + start // LANES * SUBLANES
        if lanes < LANES:
            out_ref[pl.ds(place, SUBLANES), :] = jnp.zeros((SUBLANES, LANES), jnp.float32)
        out_ref[pl.ds(place, SUBLANES), pl.ds(0, lanes)] = both[:, start : start + lanes]
    copies[chunks + 1].wait()


def stage(ref, scratch, start, middle, samples, chunks):
    for chunk in range(chunks):
        value = ref[pl.ds(chunk * samples, samples), :]
        for offset, piece in zip((0, middle), split2(value)):
            scratch[pl.ds(offset + start, samples), pl.ds(chunk * LANES, LANES)] = piece


def tail_rows(refs, samples, chunks):
    pieces = []
    for ref in refs:
        for start in range(0, samples, LANES):
            lanes = min(LANES, samples - start)
            place = samples * chunks + start // LANES * SUBLANES
            pieces.append(ref[pl.ds(place, SUBLANES), pl.ds(0, lanes)])
    return jnp.concatenate(pieces, axis=1)


def as_columns(rows):
    count = rows.shape[1]
    fill = -count % LANES
    if fill:
        rows = jnp.concatenate([rows, jnp.zeros((SUBLANES, fill), jnp.float32)], axis=1)
    return jnp.transpose(rows)[:count]


def main_kernel(samples, chunks, layout, *refs):
    places = layout.places
    queries = refs[:places]
    keys = (refs[0],) + refs[places : places + 4]
    out_ref, key_parts, query_parts, tail_ref = refs[places + 4 :]
    _, me_place, me_core = layout.here()
    rows = places * samples
    key_rows = len(keys) * samples
    group = min(GROUP_ROWS, rows)
    blocks = group // samples
    near = CORES * samples
    for place, ref in enumerate(queries):
        stage(ref, query_parts, place * samples, rows, samples, chunks)
    for place, ref in enumerate(keys):
        stage(ref, key_parts, place * samples, key_rows, samples, chunks)
    key_tail = as_columns(tail_rows(keys, samples, chunks))
    key_sign, key_norm = key_tail[:, 0:1], key_tail[:, 1:2]
    tail_ref[...] = tail_rows(queries, samples, chunks)
    lane = lax.broadcasted_iota(jnp.int32, (samples, LANES), 1)

    def one_group(index, carry):
        result, total, column = carry
        start = pl.multiple_of(index * group, group)
        both = key_parts[...]
        by_high = bf16_dot(both, query_parts[pl.ds(start, group), :], NT_DIMS)
        by_mid = bf16_dot(both, query_parts[pl.ds(rows + start, group), :], NT_DIMS)
        inner = by_high[:key_rows] + (by_high[key_rows:] + by_mid[:key_rows] + by_mid[key_rows:])
        sign = tail_ref[0:1, pl.ds(start, group)]
        norm = tail_ref[1:2, pl.ds(start, group)]
        sq_dist = norm + key_norm - 2.0 * inner
        kernel = jnp.exp(sq_dist * (-1.0 / 200.0))
        signed = kernel * key_sign
        near_sums = jnp.sum(signed[:near], axis=0, keepdims=True)
        far_sums = jnp.sum(signed[near:], axis=0, keepdims=True)
        sums = near_sums + far_sums
        total = total + jnp.sum(sign * (sums + far_sums), axis=1, keepdims=True)
        column = column + jnp.sum(kernel[near:] * sign, axis=1, keepdims=True)
        sums = as_columns(jnp.broadcast_to(sums, (SUBLANES, group)))
        for place in range(blocks):
            owner = me_place ^ (index * blocks + place)
            result = jnp.where(
                lane == owner, sums[place * samples : (place + 1) * samples, 0:1], result
            )
        return result, total, column

    carry = (
        jnp.zeros((samples, LANES), jnp.float32),
        jnp.zeros((1, 1), jnp.float32),
        jnp.zeros((FAR_BLOCKS * samples, 1), jnp.float32),
    )
    if rows == group:
        carry = one_group(0, carry)
    else:
        carry = lax.fori_loop(0, rows // group, one_group, carry)
    result, total, column = carry
    for place, offset in enumerate((me_core, 1 - me_core, 2)):
        result = jnp.where(
            lane == places + offset, column[place * samples : (place + 1) * samples], result
        )
    out_ref[...] = jnp.where(lane == places + 4, total, result)


def pick_kernel(layout, per_peer, factor, id_ref, lane_ref, row_ref):
    ids = id_ref[...]
    samples = ids.shape[1]
    places = layout.places
    plane, place, core = layout.parts(int_div(ids, samples))
    slot = int_mod(ids, per_peer)
    targets = jnp.concatenate(
        [place, places + core, jnp.full(core.shape, places + 2, jnp.int32)], axis=1
    )
    lane_of = lax.broadcasted_iota(jnp.int32, (LANES, 3 * samples), 0)
    lane_ref[...] = jnp.where(lane_of == targets, 1.0, 0.0).astype(jnp.bfloat16)
    row = lax.broadcasted_iota(jnp.int32, (samples, samples), 0)
    src_plane, src_place, src_core = layout.parts(int_div(row, per_peer))
    right_slot = int_mod(row, per_peer) == slot
    right_place = right_slot & (src_place == place)

    def sent_to(table):
        goal = jnp.full(plane.shape, -1, jnp.int32)
        for source, target in table.items():
            goal = jnp.where(plane == source, target, goal)
        return goal

    keep_row = right_slot & (src_plane == plane) & (src_core == core)
    keep_a = right_place & (src_plane == sent_to(ROUND_A))
    crossing = (plane == CROSSING[0]) | (plane == CROSSING[1])
    keep_b = right_place & (src_plane == sent_to(ROUND_B))
    keep_b = keep_b & (src_core == jnp.where(crossing, 1 - core, core))
    row_ref[...] = jnp.concatenate(
        [jnp.where(keep, factor, 0.0) for keep in (keep_row, keep_a, keep_b)], axis=1
    )


def last_kernel(layout, per_peer, scale, got_ref, lane_ref, row_ref, proof_ref, mmd_ref):
    got = got_ref[...]
    samples = got.shape[0]
    parts = jnp.concatenate(split3(got), axis=0)
    picked = bf16_dot(parts, lane_ref[...], NN_DIMS)
    picked = picked[:samples] + (picked[samples : 2 * samples] + picked[2 * samples :])
    sums = jnp.sum(picked * row_ref[...], axis=0, keepdims=True)
    proof_ref[...] = (
        sums[:, :samples] + sums[:, samples : 2 * samples] + sums[:, 2 * samples :]
    )
    row = lax.broadcasted_iota(jnp.int32, (samples, LANES), 0)
    lane = lax.broadcasted_iota(jnp.int32, (samples, LANES), 1)
    is_total = (lane == layout.places + 4) & (int_mod(row, per_peer) == 0)
    total = jnp.sum(jnp.where(is_total, got, 0.0), axis=(0, 1), keepdims=True)
    mmd_ref[...] = total * scale


def in_vmem(array):
    return pltpu.with_memory_space_constraint(array, pltpu.VMEM)


def in_hbm(array):
    return pltpu.with_memory_space_constraint(array, pltpu.HBM)


def vmem_specs(count):
    return [pl.BlockSpec(memory_space=pltpu.VMEM)] * count


def local(embeddings, labels, source_id):
    layout = Layout(lax.axis_size("row"), lax.axis_size("col"))
    places = layout.places
    samples, width = embeddings.shape
    chunks = width // LANES
    per_peer = samples // layout.devices
    half_count = samples * layout.devices // 2
    factor = 1000.0 / half_count
    tiles = -(-samples // LANES)
    pack_rows = samples * chunks + tiles * SUBLANES
    key_rows = (CORES + FAR_BLOCKS) * samples
    query_rows = places * samples
    block_bytes = pack_rows * LANES * 4
    work_bytes = (key_rows + query_rows) * width * 6 + 8 * GROUP_ROWS * key_rows * 4
    params = pltpu.CompilerParams(vmem_limit_bytes=work_bytes + 4 * MIB)

    packed, ids = pl.pallas_call(
        pack_kernel,
        out_shape=(
            pltpu.VMEM((pack_rows, LANES), jnp.float32),
            pltpu.VMEM((1, samples), jnp.int32),
        ),
        in_specs=[pl.BlockSpec(memory_space=pl.ANY)] * 3,
        out_specs=tuple(vmem_specs(2)),
        scratch_shapes=[
            pltpu.VMEM((1, samples), jnp.int32),
            pltpu.SemaphoreType.DMA((chunks + 2,)),
        ],
        compiler_params=pltpu.CompilerParams(vmem_limit_bytes=4 * block_bytes + 4 * MIB),
        name="pack_block",
    )(
        in_hbm(embeddings),
        in_hbm(labels.reshape(1, samples)),
        in_hbm(source_id.reshape(1, samples)),
    )

    def send(block, target):
        return lax.ppermute(block, ("row", "col"), layout.pairs(target))

    def round_a(plane, place, core):
        return (ROUND_A[plane], place, core)

    def round_b(plane, place, core):
        return (ROUND_B[plane], place, 1 - core if plane in CROSSING else core)

    def to_place(step):
        return lambda plane, place, core: (plane, place ^ step, core)

    def to_core(plane, place, core):
        return (plane, place, 1 - core)

    in_plane = [send(packed, to_place(step)) for step in range(1, places)]
    far_b = send(packed, round_b)
    far_a = send(packed, round_a)
    far_a_other = send(far_a, to_core)
    late, *_ = lax.optimization_barrier((packed, in_plane[-1], far_a))
    near = send(late, to_core)

    ids, far_b = lax.optimization_barrier((ids, far_b))
    lanes, rows = pl.pallas_call(
        functools.partial(pick_kernel, layout, per_peer, factor),
        out_shape=(
            pltpu.VMEM((LANES, 3 * samples), jnp.bfloat16),
            pltpu.VMEM((samples, 3 * samples), jnp.float32),
        ),
        in_specs=vmem_specs(1),
        out_specs=tuple(vmem_specs(2)),
        compiler_params=pltpu.CompilerParams(vmem_limit_bytes=16 * MIB),
        name="pick_masks",
    )(in_vmem(ids))
    far_b, lanes, rows = lax.optimization_barrier((far_b, lanes, rows))
    blocks = [packed, *in_plane, near, far_a, far_a_other, far_b]

    partial = pl.pallas_call(
        functools.partial(main_kernel, samples, chunks, layout),
        out_shape=pltpu.VMEM((samples, LANES), jnp.float32),
        in_specs=vmem_specs(len(blocks)),
        out_specs=pl.BlockSpec(memory_space=pltpu.VMEM),
        scratch_shapes=[
            pltpu.VMEM((2 * key_rows, width), jnp.bfloat16),
            pltpu.VMEM((2 * query_rows, width), jnp.bfloat16),
            pltpu.VMEM((SUBLANES, query_rows), jnp.float32),
        ],
        compiler_params=params,
        name="kernel_sums",
    )(*[in_vmem(block) for block in blocks])

    got = lax.all_to_all(partial, ("row", "col"), split_axis=0, concat_axis=0, tiled=True)

    proof, mmd = pl.pallas_call(
        functools.partial(last_kernel, layout, per_peer, factor / half_count),
        out_shape=(
            jax.ShapeDtypeStruct((1, samples), jnp.float32),
            jax.ShapeDtypeStruct((1, 1), jnp.float32),
        ),
        in_specs=vmem_specs(3),
        out_specs=tuple(vmem_specs(2)),
        compiler_params=pltpu.CompilerParams(vmem_limit_bytes=16 * MIB),
        name="pick_proof",
    )(in_vmem(got), in_vmem(lanes), in_vmem(rows))
    return proof.reshape(samples), mmd.reshape(())


def solution(mesh):
    return jax.shard_map(
        local,
        mesh=mesh,
        in_specs=(P(("row", "col"), None), P(("row", "col")), P(("row", "col"))),
        out_specs=(P(("row", "col")), P()),
        check_vma=False,
    )
```

```python
import functools

import jax
import jax.numpy as jnp
from jax import lax
from jax.experimental import pallas as pl
from jax.experimental.pallas import tpu as pltpu
from jax.sharding import PartitionSpec as P

LANES = 128
SUBLANES = 8
GROUP_ROWS = 256
PLANES = 4
CORES = 2
ROUND_A = {2: 0, 3: 1, 1: 2, 0: 3}
ROUND_B = {0: 1, 3: 2, 1: 0, 2: 3}
CROSSING = (0, 3)
FAR_BLOCKS = 3
MIB = 1024 * 1024
NT_DIMS = (((1,), (1,)), ((), ()))
NN_DIMS = (((1,), (0,)), ((), ()))


def int_div(value, divisor):
    if divisor & (divisor - 1) == 0:
        return lax.shift_right_logical(value, divisor.bit_length() - 1)
    return value // divisor


def int_mod(value, divisor):
    if divisor & (divisor - 1) == 0:
        return value & (divisor - 1)
    return value % divisor


class Layout:
    def __init__(self, row_count, col_count):
        self.core_in_row = row_count == PLANES * CORES
        self.places = col_count if self.core_in_row else col_count // CORES
        self.devices = row_count * col_count

    def flat(self, plane, place, core):
        if self.core_in_row:
            return (plane * CORES + core) * self.places + place
        return (plane * self.places + place) * CORES + core

    def parts(self, flat):
        if self.core_in_row:
            place, rest = int_mod(flat, self.places), int_div(flat, self.places)
            return int_div(rest, CORES), place, int_mod(rest, CORES)
        core, rest = int_mod(flat, CORES), int_div(flat, CORES)
        return int_div(rest, self.places), int_mod(rest, self.places), core

    def here(self):
        row, col = lax.axis_index("row"), lax.axis_index("col")
        if self.core_in_row:
            return int_div(row, CORES), col, int_mod(row, CORES)
        return row, int_div(col, CORES), int_mod(col, CORES)

    def pairs(self, target):
        result = []
        for plane in range(PLANES):
            for place in range(self.places):
                for core in range(CORES):
                    goal = target(plane, place, core)
                    result.append((self.flat(plane, place, core), self.flat(*goal)))
        return sorted(result)


def split2(value):
    high = value.astype(jnp.bfloat16)
    return high, (value - high.astype(jnp.float32)).astype(jnp.bfloat16)


def split3(value):
    high = value.astype(jnp.bfloat16)
    rest = value - high.astype(jnp.float32)
    mid = rest.astype(jnp.bfloat16)
    low = (rest - mid.astype(jnp.float32)).astype(jnp.bfloat16)
    return high, mid, low


def bf16_dot(left, right, dims):
    return lax.dot_general(left, right, dims, preferred_element_type=jnp.float32)


def pack_kernel(emb_ref, label_ref, id_ref, out_ref, id_out_ref, label_vmem, copied):
    samples, width = emb_ref.shape
    chunks = width // LANES
    copies = [
        pltpu.make_async_copy(
            emb_ref.at[:, pl.ds(chunk * LANES, LANES)],
            out_ref.at[pl.ds(chunk * samples, samples), :],
            copied.at[chunk],
        )
        for chunk in range(chunks)
    ]
    copies.append(pltpu.make_async_copy(label_ref, label_vmem, copied.at[chunks]))
    copies.append(pltpu.make_async_copy(id_ref, id_out_ref, copied.at[chunks + 1]))
    for copy in copies:
        copy.start()
    squares = jnp.zeros((samples, LANES), jnp.float32)
    for chunk in range(chunks):
        copies[chunk].wait()
        value = out_ref[pl.ds(chunk * samples, samples), :]
        squares = squares + value * value
    ones = jnp.ones((SUBLANES, LANES), jnp.bfloat16)
    high, mid, low = (bf16_dot(ones, part, NT_DIMS) for part in split3(squares))
    norm = high + (mid + low)
    copies[chunks].wait()
    sign = (1 - 2 * label_vmem[...]).astype(jnp.float32)
    base = samples * chunks
    row = lax.broadcasted_iota(jnp.int32, (SUBLANES, samples), 0)
    both = jnp.where(row == 0, sign, norm)
    for start in range(0, samples, LANES):
        lanes = min(LANES, samples - start)
        place = base + start // LANES * SUBLANES
        if lanes < LANES:
            out_ref[pl.ds(place, SUBLANES), :] = jnp.zeros((SUBLANES, LANES), jnp.float32)
        out_ref[pl.ds(place, SUBLANES), pl.ds(0, lanes)] = both[:, start : start + lanes]
    copies[chunks + 1].wait()


def stage(ref, scratch, start, order, samples, chunks):
    for chunk in range(chunks):
        pieces = split2(ref[pl.ds(chunk * samples, samples), :])
        for place, part in enumerate(order):
            lanes = pl.ds((place * chunks + chunk) * LANES, LANES)
            scratch[pl.ds(start, samples), lanes] = pieces[part]


def tail_rows(refs, samples, chunks):
    pieces = []
    for ref in refs:
        for start in range(0, samples, LANES):
            lanes = min(LANES, samples - start)
            place = samples * chunks + start // LANES * SUBLANES
            pieces.append(ref[pl.ds(place, SUBLANES), pl.ds(0, lanes)])
    return jnp.concatenate(pieces, axis=1)


def as_columns(rows):
    count = rows.shape[1]
    fill = -count % LANES
    if fill:
        rows = jnp.concatenate([rows, jnp.zeros((SUBLANES, fill), jnp.float32)], axis=1)
    return jnp.transpose(rows)[:count]


def main_kernel(samples, chunks, layout, *refs):
    places = layout.places
    queries = refs[:places]
    keys = (refs[0],) + refs[places : places + 4]
    out_ref, key_parts, query_parts, tail_ref = refs[places + 4 :]
    _, me_place, me_core = layout.here()
    rows = places * samples
    group = min(GROUP_ROWS, rows)
    blocks = group // samples
    near = CORES * samples
    for place, ref in enumerate(queries):
        stage(ref, query_parts, place * samples, (0, 0, 1, 1), samples, chunks)
    for place, ref in enumerate(keys):
        stage(ref, key_parts, place * samples, (0, 1, 0, 1), samples, chunks)
    key_tail = as_columns(tail_rows(keys, samples, chunks))
    key_sign, key_norm = key_tail[:, 0:1], key_tail[:, 1:2]
    tail_ref[...] = tail_rows(queries, samples, chunks)
    lane = lax.broadcasted_iota(jnp.int32, (samples, LANES), 1)

    def one_group(index, carry):
        result, total, column = carry
        start = pl.multiple_of(index * group, group)
        inner = bf16_dot(key_parts[...], query_parts[pl.ds(start, group), :], NT_DIMS)
        sign = tail_ref[0:1, pl.ds(start, group)]
        norm = tail_ref[1:2, pl.ds(start, group)]
        sq_dist = norm + key_norm - 2.0 * inner
        kernel = jnp.exp(sq_dist * (-1.0 / 200.0))
        signed = kernel * key_sign
        near_sums = jnp.sum(signed[:near], axis=0, keepdims=True)
        far_sums = jnp.sum(signed[near:], axis=0, keepdims=True)
        sums = near_sums + far_sums
        total = total + jnp.sum(sign * (sums + far_sums), axis=1, keepdims=True)
        column = column + jnp.sum(kernel[near:] * sign, axis=1, keepdims=True)
        sums = as_columns(jnp.broadcast_to(sums, (SUBLANES, group)))
        for place in range(blocks):
            owner = me_place ^ (index * blocks + place)
            result = jnp.where(
                lane == owner, sums[place * samples : (place + 1) * samples, 0:1], result
            )
        return result, total, column

    carry = (
        jnp.zeros((samples, LANES), jnp.float32),
        jnp.zeros((1, 1), jnp.float32),
        jnp.zeros((FAR_BLOCKS * samples, 1), jnp.float32),
    )
    if rows == group:
        carry = one_group(0, carry)
    else:
        carry = lax.fori_loop(0, rows // group, one_group, carry)
    result, total, column = carry
    for place, offset in enumerate((me_core, 1 - me_core, 2)):
        result = jnp.where(
            lane == places + offset, column[place * samples : (place + 1) * samples], result
        )
    out_ref[...] = jnp.where(lane == places + 4, total, result)


def pick_kernel(layout, per_peer, factor, id_ref, lane_ref, row_ref):
    ids = id_ref[...]
    samples = ids.shape[1]
    places = layout.places
    plane, place, core = layout.parts(int_div(ids, samples))
    slot = int_mod(ids, per_peer)
    targets = jnp.concatenate(
        [place, places + core, jnp.full(core.shape, places + 2, jnp.int32)], axis=1
    )
    lane_of = lax.broadcasted_iota(jnp.int32, (LANES, 3 * samples), 0)
    lane_ref[...] = jnp.where(lane_of == targets, 1.0, 0.0).astype(jnp.bfloat16)
    row = lax.broadcasted_iota(jnp.int32, (samples, samples), 0)
    src_plane, src_place, src_core = layout.parts(int_div(row, per_peer))
    right_slot = int_mod(row, per_peer) == slot
    right_place = right_slot & (src_place == place)

    def sent_to(table):
        goal = jnp.full(plane.shape, -1, jnp.int32)
        for source, target in table.items():
            goal = jnp.where(plane == source, target, goal)
        return goal

    keep_row = right_slot & (src_plane == plane) & (src_core == core)
    keep_a = right_place & (src_plane == sent_to(ROUND_A))
    crossing = (plane == CROSSING[0]) | (plane == CROSSING[1])
    keep_b = right_place & (src_plane == sent_to(ROUND_B))
    keep_b = keep_b & (src_core == jnp.where(crossing, 1 - core, core))
    row_ref[...] = jnp.concatenate(
        [jnp.where(keep, factor, 0.0) for keep in (keep_row, keep_a, keep_b)], axis=1
    )


def last_kernel(layout, per_peer, scale, got_ref, lane_ref, row_ref, proof_ref, mmd_ref):
    got = got_ref[...]
    samples = got.shape[0]
    parts = jnp.concatenate(split3(got), axis=0)
    picked = bf16_dot(parts, lane_ref[...], NN_DIMS)
    picked = picked[:samples] + (picked[samples : 2 * samples] + picked[2 * samples :])
    sums = jnp.sum(picked * row_ref[...], axis=0, keepdims=True)
    proof_ref[...] = (
        sums[:, :samples] + sums[:, samples : 2 * samples] + sums[:, 2 * samples :]
    )
    row = lax.broadcasted_iota(jnp.int32, (samples, LANES), 0)
    lane = lax.broadcasted_iota(jnp.int32, (samples, LANES), 1)
    is_total = (lane == layout.places + 4) & (int_mod(row, per_peer) == 0)
    total = jnp.sum(jnp.where(is_total, got, 0.0), axis=(0, 1), keepdims=True)
    mmd_ref[...] = total * scale


def in_vmem(array):
    return pltpu.with_memory_space_constraint(array, pltpu.VMEM)


def in_hbm(array):
    return pltpu.with_memory_space_constraint(array, pltpu.HBM)


def vmem_specs(count):
    return [pl.BlockSpec(memory_space=pltpu.VMEM)] * count


def local(embeddings, labels, source_id):
    layout = Layout(lax.axis_size("row"), lax.axis_size("col"))
    places = layout.places
    samples, width = embeddings.shape
    chunks = width // LANES
    per_peer = samples // layout.devices
    half_count = samples * layout.devices // 2
    factor = 1000.0 / half_count
    tiles = -(-samples // LANES)
    pack_rows = samples * chunks + tiles * SUBLANES
    key_rows = (CORES + FAR_BLOCKS) * samples
    query_rows = places * samples
    block_bytes = pack_rows * LANES * 4
    work_bytes = (key_rows + query_rows) * width * 8 + 4 * GROUP_ROWS * key_rows * 4
    params = pltpu.CompilerParams(vmem_limit_bytes=work_bytes + 4 * MIB)

    packed, ids = pl.pallas_call(
        pack_kernel,
        out_shape=(
            pltpu.VMEM((pack_rows, LANES), jnp.float32),
            pltpu.VMEM((1, samples), jnp.int32),
        ),
        in_specs=[pl.BlockSpec(memory_space=pl.ANY)] * 3,
        out_specs=tuple(vmem_specs(2)),
        scratch_shapes=[
            pltpu.VMEM((1, samples), jnp.int32),
            pltpu.SemaphoreType.DMA((chunks + 2,)),
        ],
        compiler_params=pltpu.CompilerParams(vmem_limit_bytes=4 * block_bytes + 4 * MIB),
        name="pack_block",
    )(
        in_hbm(embeddings),
        in_hbm(labels.reshape(1, samples)),
        in_hbm(source_id.reshape(1, samples)),
    )

    def send(block, target):
        return lax.ppermute(block, ("row", "col"), layout.pairs(target))

    def round_a(plane, place, core):
        return (ROUND_A[plane], place, core)

    def round_b(plane, place, core):
        return (ROUND_B[plane], place, 1 - core if plane in CROSSING else core)

    def to_place(step):
        return lambda plane, place, core: (plane, place ^ step, core)

    def to_core(plane, place, core):
        return (plane, place, 1 - core)

    in_plane = [send(packed, to_place(step)) for step in range(1, places)]
    far_b = send(packed, round_b)
    far_a = send(packed, round_a)
    far_a_other = send(far_a, to_core)
    late, *_ = lax.optimization_barrier((packed, in_plane[-1], far_a))
    near = send(late, to_core)

    ids, far_b = lax.optimization_barrier((ids, far_b))
    lanes, rows = pl.pallas_call(
        functools.partial(pick_kernel, layout, per_peer, factor),
        out_shape=(
            pltpu.VMEM((LANES, 3 * samples), jnp.bfloat16),
            pltpu.VMEM((samples, 3 * samples), jnp.float32),
        ),
        in_specs=vmem_specs(1),
        out_specs=tuple(vmem_specs(2)),
        compiler_params=pltpu.CompilerParams(vmem_limit_bytes=16 * MIB),
        name="pick_masks",
    )(in_vmem(ids))
    far_b, lanes, rows = lax.optimization_barrier((far_b, lanes, rows))
    blocks = [packed, *in_plane, near, far_a, far_a_other, far_b]

    partial = pl.pallas_call(
        functools.partial(main_kernel, samples, chunks, layout),
        out_shape=pltpu.VMEM((samples, LANES), jnp.float32),
        in_specs=vmem_specs(len(blocks)),
        out_specs=pl.BlockSpec(memory_space=pltpu.VMEM),
        scratch_shapes=[
            pltpu.VMEM((key_rows, 4 * width), jnp.bfloat16),
            pltpu.VMEM((query_rows, 4 * width), jnp.bfloat16),
            pltpu.VMEM((SUBLANES, query_rows), jnp.float32),
        ],
        compiler_params=params,
        name="kernel_sums",
    )(*[in_vmem(block) for block in blocks])

    got = lax.all_to_all(partial, ("row", "col"), split_axis=0, concat_axis=0, tiled=True)

    proof, mmd = pl.pallas_call(
        functools.partial(last_kernel, layout, per_peer, factor / half_count),
        out_shape=(
            jax.ShapeDtypeStruct((1, samples), jnp.float32),
            jax.ShapeDtypeStruct((1, 1), jnp.float32),
        ),
        in_specs=vmem_specs(3),
        out_specs=tuple(vmem_specs(2)),
        compiler_params=pltpu.CompilerParams(vmem_limit_bytes=16 * MIB),
        name="pick_proof",
    )(in_vmem(got), in_vmem(lanes), in_vmem(rows))
    return proof.reshape(samples), mmd.reshape(())


def solution(mesh):
    return jax.shard_map(
        local,
        mesh=mesh,
        in_specs=(P(("row", "col"), None), P(("row", "col")), P(("row", "col"))),
        out_specs=(P(("row", "col")), P()),
        check_vma=False,
    )
```

```python
import functools

import jax
import jax.numpy as jnp
from jax import lax
from jax.experimental import pallas as pl
from jax.experimental.pallas import tpu as pltpu
from jax.sharding import PartitionSpec as P

LANES = 128
SUBLANES = 8
GROUP_ROWS = 256
PLANES = 4
CORES = 2
ROUND_A = {2: 0, 3: 1, 1: 2, 0: 3}
ROUND_B = {0: 1, 3: 2, 1: 0, 2: 3}
CROSSING = (0, 3)
FAR_BLOCKS = 3
MIB = 1024 * 1024
NT_DIMS = (((1,), (1,)), ((), ()))
NN_DIMS = (((1,), (0,)), ((), ()))


def int_div(value, divisor):
    if divisor & (divisor - 1) == 0:
        return lax.shift_right_logical(value, divisor.bit_length() - 1)
    return value // divisor


def int_mod(value, divisor):
    if divisor & (divisor - 1) == 0:
        return value & (divisor - 1)
    return value % divisor


class Layout:
    def __init__(self, row_count, col_count):
        self.core_in_row = row_count == PLANES * CORES
        self.places = col_count if self.core_in_row else col_count // CORES
        self.devices = row_count * col_count

    def flat(self, plane, place, core):
        if self.core_in_row:
            return (plane * CORES + core) * self.places + place
        return (plane * self.places + place) * CORES + core

    def parts(self, flat):
        if self.core_in_row:
            place, rest = int_mod(flat, self.places), int_div(flat, self.places)
            return int_div(rest, CORES), place, int_mod(rest, CORES)
        core, rest = int_mod(flat, CORES), int_div(flat, CORES)
        return int_div(rest, self.places), int_mod(rest, self.places), core

    def here(self):
        row, col = lax.axis_index("row"), lax.axis_index("col")
        if self.core_in_row:
            return int_div(row, CORES), col, int_mod(row, CORES)
        return row, int_div(col, CORES), int_mod(col, CORES)

    def pairs(self, target):
        result = []
        for plane in range(PLANES):
            for place in range(self.places):
                for core in range(CORES):
                    goal = target(plane, place, core)
                    result.append((self.flat(plane, place, core), self.flat(*goal)))
        return sorted(result)


def split2(value):
    high = value.astype(jnp.bfloat16)
    return high, (value - high.astype(jnp.float32)).astype(jnp.bfloat16)


def split3(value):
    high = value.astype(jnp.bfloat16)
    rest = value - high.astype(jnp.float32)
    mid = rest.astype(jnp.bfloat16)
    low = (rest - mid.astype(jnp.float32)).astype(jnp.bfloat16)
    return high, mid, low


def bf16_dot(left, right, dims):
    return lax.dot_general(left, right, dims, preferred_element_type=jnp.float32)


def pack_kernel(emb_ref, label_ref, id_ref, out_ref, id_out_ref, label_vmem, copied):
    samples, width = emb_ref.shape
    chunks = width // LANES
    copies = [
        pltpu.make_async_copy(
            emb_ref.at[:, pl.ds(chunk * LANES, LANES)],
            out_ref.at[pl.ds(chunk * samples, samples), :],
            copied.at[chunk],
        )
        for chunk in range(chunks)
    ]
    copies.append(pltpu.make_async_copy(label_ref, label_vmem, copied.at[chunks]))
    copies.append(pltpu.make_async_copy(id_ref, id_out_ref, copied.at[chunks + 1]))
    for copy in copies:
        copy.start()
    squares = jnp.zeros((samples, LANES), jnp.float32)
    for chunk in range(chunks):
        copies[chunk].wait()
        value = out_ref[pl.ds(chunk * samples, samples), :]
        squares = squares + value * value
    ones = jnp.ones((SUBLANES, LANES), jnp.bfloat16)
    high, mid, low = (bf16_dot(ones, part, NT_DIMS) for part in split3(squares))
    norm = high + (mid + low)
    copies[chunks].wait()
    sign = (1 - 2 * label_vmem[...]).astype(jnp.float32)
    base = samples * chunks
    row = lax.broadcasted_iota(jnp.int32, (SUBLANES, samples), 0)
    both = jnp.where(row == 0, sign, norm)
    for start in range(0, samples, LANES):
        lanes = min(LANES, samples - start)
        place = base + start // LANES * SUBLANES
        if lanes < LANES:
            out_ref[pl.ds(place, SUBLANES), :] = jnp.zeros((SUBLANES, LANES), jnp.float32)
        out_ref[pl.ds(place, SUBLANES), pl.ds(0, lanes)] = both[:, start : start + lanes]
    copies[chunks + 1].wait()


def stage(ref, scratch, start, middle, samples, chunks):
    for chunk in range(chunks):
        value = ref[pl.ds(chunk * samples, samples), :]
        for offset, piece in zip((0, middle), split2(value)):
            scratch[pl.ds(offset + start, samples), pl.ds(chunk * LANES, LANES)] = piece


def tail_rows(refs, samples, chunks):
    pieces = []
    for ref in refs:
        for start in range(0, samples, LANES):
            lanes = min(LANES, samples - start)
            place = samples * chunks + start // LANES * SUBLANES
            pieces.append(ref[pl.ds(place, SUBLANES), pl.ds(0, lanes)])
    return jnp.concatenate(pieces, axis=1)


def as_columns(rows):
    count = rows.shape[1]
    fill = -count % LANES
    if fill:
        rows = jnp.concatenate([rows, jnp.zeros((SUBLANES, fill), jnp.float32)], axis=1)
    return jnp.transpose(rows)[:count]


def main_kernel(samples, chunks, layout, *refs):
    places = layout.places
    queries = refs[:places]
    keys = (refs[0],) + refs[places : places + 4]
    out_ref, key_parts, query_parts, tail_ref = refs[places + 4 :]
    _, me_place, me_core = layout.here()
    rows = places * samples
    key_rows = len(keys) * samples
    group = min(GROUP_ROWS, rows)
    blocks = group // samples
    near = CORES * samples
    for place, ref in enumerate(queries):
        stage(ref, query_parts, place * samples, rows, samples, chunks)
    for place, ref in enumerate(keys):
        stage(ref, key_parts, place * samples, key_rows, samples, chunks)
    key_tail = as_columns(tail_rows(keys, samples, chunks))
    key_sign, key_norm = key_tail[:, 0:1], key_tail[:, 1:2]
    tail_ref[...] = tail_rows(queries, samples, chunks)
    lane = lax.broadcasted_iota(jnp.int32, (samples, LANES), 1)

    def one_group(index, carry):
        result, total, column = carry
        start = pl.multiple_of(index * group, group)
        both = key_parts[...]
        by_high = bf16_dot(both, query_parts[pl.ds(start, group), :], NT_DIMS)
        by_mid = bf16_dot(both, query_parts[pl.ds(rows + start, group), :], NT_DIMS)
        inner = by_high[:key_rows] + (by_high[key_rows:] + by_mid[:key_rows] + by_mid[key_rows:])
        sign = tail_ref[0:1, pl.ds(start, group)]
        norm = tail_ref[1:2, pl.ds(start, group)]
        sq_dist = norm + key_norm - 2.0 * inner
        kernel = jnp.exp(sq_dist * (-1.0 / 200.0))
        signed = kernel * key_sign
        near_sums = jnp.sum(signed[:near], axis=0, keepdims=True)
        far_sums = jnp.sum(signed[near:], axis=0, keepdims=True)
        sums = near_sums + far_sums
        total = total + jnp.sum(sign * (sums + far_sums), axis=1, keepdims=True)
        column = column + jnp.sum(kernel[near:] * sign, axis=1, keepdims=True)
        sums = as_columns(jnp.broadcast_to(sums, (SUBLANES, group)))
        for place in range(blocks):
            owner = me_place ^ (index * blocks + place)
            result = jnp.where(
                lane == owner, sums[place * samples : (place + 1) * samples, 0:1], result
            )
        return result, total, column

    carry = (
        jnp.zeros((samples, LANES), jnp.float32),
        jnp.zeros((1, 1), jnp.float32),
        jnp.zeros((FAR_BLOCKS * samples, 1), jnp.float32),
    )
    if rows == group:
        carry = one_group(0, carry)
    else:
        carry = lax.fori_loop(0, rows // group, one_group, carry)
    result, total, column = carry
    for place, offset in enumerate((me_core, 1 - me_core, 2)):
        result = jnp.where(
            lane == places + offset, column[place * samples : (place + 1) * samples], result
        )
    out_ref[...] = jnp.where(lane == places + 4, total, result)


def pick_kernel(layout, per_peer, factor, id_ref, lane_ref, row_ref):
    ids = id_ref[...]
    samples = ids.shape[1]
    places = layout.places
    plane, place, core = layout.parts(int_div(ids, samples))
    slot = int_mod(ids, per_peer)
    targets = jnp.concatenate(
        [place, places + core, jnp.full(core.shape, places + 2, jnp.int32)], axis=1
    )
    lane_of = lax.broadcasted_iota(jnp.int32, (LANES, 3 * samples), 0)
    lane_ref[...] = jnp.where(lane_of == targets, 1.0, 0.0).astype(jnp.bfloat16)
    row = lax.broadcasted_iota(jnp.int32, (samples, samples), 0)
    src_plane, src_place, src_core = layout.parts(int_div(row, per_peer))
    right_slot = int_mod(row, per_peer) == slot
    right_place = right_slot & (src_place == place)

    def sent_to(table):
        goal = jnp.full(plane.shape, -1, jnp.int32)
        for source, target in table.items():
            goal = jnp.where(plane == source, target, goal)
        return goal

    keep_row = right_slot & (src_plane == plane) & (src_core == core)
    keep_a = right_place & (src_plane == sent_to(ROUND_A))
    crossing = (plane == CROSSING[0]) | (plane == CROSSING[1])
    keep_b = right_place & (src_plane == sent_to(ROUND_B))
    keep_b = keep_b & (src_core == jnp.where(crossing, 1 - core, core))
    row_ref[...] = jnp.concatenate(
        [jnp.where(keep, factor, 0.0) for keep in (keep_row, keep_a, keep_b)], axis=1
    )


def last_kernel(layout, per_peer, scale, got_ref, lane_ref, row_ref, proof_ref, mmd_ref):
    got = got_ref[...]
    samples = got.shape[0]
    parts = jnp.concatenate(split3(got), axis=0)
    picked = bf16_dot(parts, lane_ref[...], NN_DIMS)
    picked = picked[:samples] + (picked[samples : 2 * samples] + picked[2 * samples :])
    sums = jnp.sum(picked * row_ref[...], axis=0, keepdims=True)
    proof_ref[...] = (
        sums[:, :samples] + sums[:, samples : 2 * samples] + sums[:, 2 * samples :]
    )
    row = lax.broadcasted_iota(jnp.int32, (samples, LANES), 0)
    lane = lax.broadcasted_iota(jnp.int32, (samples, LANES), 1)
    is_total = (lane == layout.places + 4) & (int_mod(row, per_peer) == 0)
    total = jnp.sum(jnp.where(is_total, got, 0.0), axis=(0, 1), keepdims=True)
    mmd_ref[...] = total * scale


def in_vmem(array):
    return pltpu.with_memory_space_constraint(array, pltpu.VMEM)


def in_hbm(array):
    return pltpu.with_memory_space_constraint(array, pltpu.HBM)


def vmem_specs(count):
    return [pl.BlockSpec(memory_space=pltpu.VMEM)] * count


def local(embeddings, labels, source_id):
    layout = Layout(lax.axis_size("row"), lax.axis_size("col"))
    places = layout.places
    samples, width = embeddings.shape
    chunks = width // LANES
    per_peer = samples // layout.devices
    half_count = samples * layout.devices // 2
    factor = 1000.0 / half_count
    tiles = -(-samples // LANES)
    pack_rows = samples * chunks + tiles * SUBLANES
    key_rows = (CORES + FAR_BLOCKS) * samples
    query_rows = places * samples
    block_bytes = pack_rows * LANES * 4
    work_bytes = (key_rows + query_rows) * width * 6 + 8 * GROUP_ROWS * key_rows * 4
    params = pltpu.CompilerParams(vmem_limit_bytes=work_bytes + 4 * MIB)

    packed, ids = pl.pallas_call(
        pack_kernel,
        out_shape=(
            pltpu.VMEM((pack_rows, LANES), jnp.float32),
            pltpu.VMEM((1, samples), jnp.int32),
        ),
        in_specs=[pl.BlockSpec(memory_space=pl.ANY)] * 3,
        out_specs=tuple(vmem_specs(2)),
        scratch_shapes=[
            pltpu.VMEM((1, samples), jnp.int32),
            pltpu.SemaphoreType.DMA((chunks + 2,)),
        ],
        compiler_params=pltpu.CompilerParams(vmem_limit_bytes=4 * block_bytes + 4 * MIB),
        name="pack_block",
    )(
        in_hbm(embeddings),
        in_hbm(labels.reshape(1, samples)),
        in_hbm(source_id.reshape(1, samples)),
    )

    def send(block, target):
        return lax.ppermute(block, ("row", "col"), layout.pairs(target))

    def round_a(plane, place, core):
        return (ROUND_A[plane], place, core)

    def round_b(plane, place, core):
        return (ROUND_B[plane], place, 1 - core if plane in CROSSING else core)

    def to_place(step):
        return lambda plane, place, core: (plane, place ^ step, core)

    def to_core(plane, place, core):
        return (plane, place, 1 - core)

    in_plane = [send(packed, to_place(step)) for step in range(1, places)]
    far_b = send(packed, round_b)
    far_a = send(packed, round_a)
    late_a, *_ = lax.optimization_barrier((far_a, in_plane[1]))
    far_a_other = send(late_a, to_core)
    late, *_ = lax.optimization_barrier((packed, in_plane[1]))
    near = send(late, to_core)

    ids, far_b = lax.optimization_barrier((ids, far_b))
    lanes, rows = pl.pallas_call(
        functools.partial(pick_kernel, layout, per_peer, factor),
        out_shape=(
            pltpu.VMEM((LANES, 3 * samples), jnp.bfloat16),
            pltpu.VMEM((samples, 3 * samples), jnp.float32),
        ),
        in_specs=vmem_specs(1),
        out_specs=tuple(vmem_specs(2)),
        compiler_params=pltpu.CompilerParams(vmem_limit_bytes=16 * MIB),
        name="pick_masks",
    )(in_vmem(ids))
    far_b, lanes, rows = lax.optimization_barrier((far_b, lanes, rows))
    blocks = [packed, *in_plane, near, far_a, far_a_other, far_b]

    partial = pl.pallas_call(
        functools.partial(main_kernel, samples, chunks, layout),
        out_shape=pltpu.VMEM((samples, LANES), jnp.float32),
        in_specs=vmem_specs(len(blocks)),
        out_specs=pl.BlockSpec(memory_space=pltpu.VMEM),
        scratch_shapes=[
            pltpu.VMEM((2 * key_rows, width), jnp.bfloat16),
            pltpu.VMEM((2 * query_rows, width), jnp.bfloat16),
            pltpu.VMEM((SUBLANES, query_rows), jnp.float32),
        ],
        compiler_params=params,
        name="kernel_sums",
    )(*[in_vmem(block) for block in blocks])

    got = lax.all_to_all(partial, ("row", "col"), split_axis=0, concat_axis=0, tiled=True)

    proof, mmd = pl.pallas_call(
        functools.partial(last_kernel, layout, per_peer, factor / half_count),
        out_shape=(
            jax.ShapeDtypeStruct((1, samples), jnp.float32),
            jax.ShapeDtypeStruct((1, 1), jnp.float32),
        ),
        in_specs=vmem_specs(3),
        out_specs=tuple(vmem_specs(2)),
        compiler_params=pltpu.CompilerParams(vmem_limit_bytes=16 * MIB),
        name="pick_proof",
    )(in_vmem(got), in_vmem(lanes), in_vmem(rows))
    return proof.reshape(samples), mmd.reshape(())


def solution(mesh):
    return jax.shard_map(
        local,
        mesh=mesh,
        in_specs=(P(("row", "col"), None), P(("row", "col")), P(("row", "col"))),
        out_specs=(P(("row", "col")), P()),
        check_vma=False,
    )
```

```python
import functools

import jax
import jax.numpy as jnp
from jax import lax
from jax.experimental import pallas as pl
from jax.experimental.pallas import tpu as pltpu
from jax.sharding import PartitionSpec as P

LANES = 128
SUBLANES = 8
GROUP_ROWS = 256
PLANES = 4
CORES = 2
ROUND_A = {2: 0, 3: 1, 1: 2, 0: 3}
ROUND_B = {0: 1, 3: 2, 1: 0, 2: 3}
CROSSING = (1, 3)
FAR_BLOCKS = 3
MIB = 1024 * 1024
NT_DIMS = (((1,), (1,)), ((), ()))
NN_DIMS = (((1,), (0,)), ((), ()))


def int_div(value, divisor):
    if divisor & (divisor - 1) == 0:
        return lax.shift_right_logical(value, divisor.bit_length() - 1)
    return value // divisor


def int_mod(value, divisor):
    if divisor & (divisor - 1) == 0:
        return value & (divisor - 1)
    return value % divisor


class Layout:
    def __init__(self, row_count, col_count):
        self.core_in_row = row_count == PLANES * CORES
        self.places = col_count if self.core_in_row else col_count // CORES
        self.devices = row_count * col_count

    def flat(self, plane, place, core):
        if self.core_in_row:
            return (plane * CORES + core) * self.places + place
        return (plane * self.places + place) * CORES + core

    def parts(self, flat):
        if self.core_in_row:
            place, rest = int_mod(flat, self.places), int_div(flat, self.places)
            return int_div(rest, CORES), place, int_mod(rest, CORES)
        core, rest = int_mod(flat, CORES), int_div(flat, CORES)
        return int_div(rest, self.places), int_mod(rest, self.places), core

    def here(self):
        row, col = lax.axis_index("row"), lax.axis_index("col")
        if self.core_in_row:
            return int_div(row, CORES), col, int_mod(row, CORES)
        return row, int_div(col, CORES), int_mod(col, CORES)

    def pairs(self, target):
        result = []
        for plane in range(PLANES):
            for place in range(self.places):
                for core in range(CORES):
                    goal = target(plane, place, core)
                    result.append((self.flat(plane, place, core), self.flat(*goal)))
        return sorted(result)


def split2(value):
    high = value.astype(jnp.bfloat16)
    return high, (value - high.astype(jnp.float32)).astype(jnp.bfloat16)


def split3(value):
    high = value.astype(jnp.bfloat16)
    rest = value - high.astype(jnp.float32)
    mid = rest.astype(jnp.bfloat16)
    low = (rest - mid.astype(jnp.float32)).astype(jnp.bfloat16)
    return high, mid, low


def bf16_dot(left, right, dims):
    return lax.dot_general(left, right, dims, preferred_element_type=jnp.float32)


def pack_kernel(emb_ref, label_ref, id_ref, out_ref, id_out_ref, label_vmem, copied):
    samples, width = emb_ref.shape
    chunks = width // LANES
    copies = [
        pltpu.make_async_copy(
            emb_ref.at[:, pl.ds(chunk * LANES, LANES)],
            out_ref.at[pl.ds(chunk * samples, samples), :],
            copied.at[chunk],
        )
        for chunk in range(chunks)
    ]
    copies.append(pltpu.make_async_copy(label_ref, label_vmem, copied.at[chunks]))
    copies.append(pltpu.make_async_copy(id_ref, id_out_ref, copied.at[chunks + 1]))
    for copy in copies:
        copy.start()
    squares = jnp.zeros((samples, LANES), jnp.float32)
    for chunk in range(chunks):
        copies[chunk].wait()
        value = out_ref[pl.ds(chunk * samples, samples), :]
        squares = squares + value * value
    ones = jnp.ones((SUBLANES, LANES), jnp.bfloat16)
    high, mid, low = (bf16_dot(ones, part, NT_DIMS) for part in split3(squares))
    norm = high + (mid + low)
    copies[chunks].wait()
    sign = (1 - 2 * label_vmem[...]).astype(jnp.float32)
    base = samples * chunks
    row = lax.broadcasted_iota(jnp.int32, (SUBLANES, samples), 0)
    both = jnp.where(row == 0, sign, norm)
    for start in range(0, samples, LANES):
        lanes = min(LANES, samples - start)
        place = base + start // LANES * SUBLANES
        if lanes < LANES:
            out_ref[pl.ds(place, SUBLANES), :] = jnp.zeros((SUBLANES, LANES), jnp.float32)
        out_ref[pl.ds(place, SUBLANES), pl.ds(0, lanes)] = both[:, start : start + lanes]
    copies[chunks + 1].wait()


def stage(ref, scratch, start, middle, samples, chunks):
    for chunk in range(chunks):
        value = ref[pl.ds(chunk * samples, samples), :]
        for offset, piece in zip((0, middle), split2(value)):
            scratch[pl.ds(offset + start, samples), pl.ds(chunk * LANES, LANES)] = piece


def tail_rows(refs, samples, chunks):
    pieces = []
    for ref in refs:
        for start in range(0, samples, LANES):
            lanes = min(LANES, samples - start)
            place = samples * chunks + start // LANES * SUBLANES
            pieces.append(ref[pl.ds(place, SUBLANES), pl.ds(0, lanes)])
    return jnp.concatenate(pieces, axis=1)


def as_columns(rows):
    count = rows.shape[1]
    fill = -count % LANES
    if fill:
        rows = jnp.concatenate([rows, jnp.zeros((SUBLANES, fill), jnp.float32)], axis=1)
    return jnp.transpose(rows)[:count]


def main_kernel(samples, chunks, layout, *refs):
    places = layout.places
    queries = refs[:places]
    keys = (refs[0],) + refs[places : places + 4]
    out_ref, key_parts, query_parts, tail_ref = refs[places + 4 :]
    _, me_place, me_core = layout.here()
    rows = places * samples
    key_rows = len(keys) * samples
    group = min(GROUP_ROWS, rows)
    blocks = group // samples
    near = CORES * samples
    for place, ref in enumerate(queries):
        stage(ref, query_parts, place * samples, rows, samples, chunks)
    for place, ref in enumerate(keys):
        stage(ref, key_parts, place * samples, key_rows, samples, chunks)
    key_tail = as_columns(tail_rows(keys, samples, chunks))
    key_sign, key_norm = key_tail[:, 0:1], key_tail[:, 1:2]
    tail_ref[...] = tail_rows(queries, samples, chunks)
    lane = lax.broadcasted_iota(jnp.int32, (samples, LANES), 1)

    def one_group(index, carry):
        result, total, column = carry
        start = pl.multiple_of(index * group, group)
        both = key_parts[...]
        by_high = bf16_dot(both, query_parts[pl.ds(start, group), :], NT_DIMS)
        by_mid = bf16_dot(both, query_parts[pl.ds(rows + start, group), :], NT_DIMS)
        inner = by_high[:key_rows] + (by_high[key_rows:] + by_mid[:key_rows] + by_mid[key_rows:])
        sign = tail_ref[0:1, pl.ds(start, group)]
        norm = tail_ref[1:2, pl.ds(start, group)]
        sq_dist = norm + key_norm - 2.0 * inner
        kernel = jnp.exp(sq_dist * (-1.0 / 200.0))
        signed = kernel * key_sign
        near_sums = jnp.sum(signed[:near], axis=0, keepdims=True)
        far_sums = jnp.sum(signed[near:], axis=0, keepdims=True)
        sums = near_sums + far_sums
        total = total + jnp.sum(sign * (sums + far_sums), axis=1, keepdims=True)
        column = column + jnp.sum(kernel[near:] * sign, axis=1, keepdims=True)
        sums = as_columns(jnp.broadcast_to(sums, (SUBLANES, group)))
        for place in range(blocks):
            owner = me_place ^ (index * blocks + place)
            result = jnp.where(
                lane == owner, sums[place * samples : (place + 1) * samples, 0:1], result
            )
        return result, total, column

    carry = (
        jnp.zeros((samples, LANES), jnp.float32),
        jnp.zeros((1, 1), jnp.float32),
        jnp.zeros((FAR_BLOCKS * samples, 1), jnp.float32),
    )
    if rows == group:
        carry = one_group(0, carry)
    else:
        carry = lax.fori_loop(0, rows // group, one_group, carry)
    result, total, column = carry
    for place, offset in enumerate((me_core, 1 - me_core, 2)):
        result = jnp.where(
            lane == places + offset, column[place * samples : (place + 1) * samples], result
        )
    out_ref[...] = jnp.where(lane == places + 4, total, result)


def pick_kernel(layout, per_peer, factor, id_ref, lane_ref, row_ref):
    ids = id_ref[...]
    samples = ids.shape[1]
    places = layout.places
    plane, place, core = layout.parts(int_div(ids, samples))
    slot = int_mod(ids, per_peer)
    targets = jnp.concatenate(
        [place, places + core, jnp.full(core.shape, places + 2, jnp.int32)], axis=1
    )
    lane_of = lax.broadcasted_iota(jnp.int32, (LANES, 3 * samples), 0)
    lane_ref[...] = jnp.where(lane_of == targets, 1.0, 0.0).astype(jnp.bfloat16)
    row = lax.broadcasted_iota(jnp.int32, (samples, samples), 0)
    src_plane, src_place, src_core = layout.parts(int_div(row, per_peer))
    right_slot = int_mod(row, per_peer) == slot
    right_place = right_slot & (src_place == place)

    def sent_to(table):
        goal = jnp.full(plane.shape, -1, jnp.int32)
        for source, target in table.items():
            goal = jnp.where(plane == source, target, goal)
        return goal

    keep_row = right_slot & (src_plane == plane) & (src_core == core)
    keep_a = right_place & (src_plane == sent_to(ROUND_A))
    crossing = (plane == CROSSING[0]) | (plane == CROSSING[1])
    keep_b = right_place & (src_plane == sent_to(ROUND_B))
    keep_b = keep_b & (src_core == jnp.where(crossing, 1 - core, core))
    row_ref[...] = jnp.concatenate(
        [jnp.where(keep, factor, 0.0) for keep in (keep_row, keep_a, keep_b)], axis=1
    )


def last_kernel(layout, per_peer, scale, got_ref, lane_ref, row_ref, proof_ref, mmd_ref):
    got = got_ref[...]
    samples = got.shape[0]
    parts = jnp.concatenate(split3(got), axis=0)
    picked = bf16_dot(parts, lane_ref[...], NN_DIMS)
    picked = picked[:samples] + (picked[samples : 2 * samples] + picked[2 * samples :])
    sums = jnp.sum(picked * row_ref[...], axis=0, keepdims=True)
    proof_ref[...] = (
        sums[:, :samples] + sums[:, samples : 2 * samples] + sums[:, 2 * samples :]
    )
    row = lax.broadcasted_iota(jnp.int32, (samples, LANES), 0)
    lane = lax.broadcasted_iota(jnp.int32, (samples, LANES), 1)
    is_total = (lane == layout.places + 4) & (int_mod(row, per_peer) == 0)
    total = jnp.sum(jnp.where(is_total, got, 0.0), axis=(0, 1), keepdims=True)
    mmd_ref[...] = total * scale


def in_vmem(array):
    return pltpu.with_memory_space_constraint(array, pltpu.VMEM)


def in_hbm(array):
    return pltpu.with_memory_space_constraint(array, pltpu.HBM)


def vmem_specs(count):
    return [pl.BlockSpec(memory_space=pltpu.VMEM)] * count


def local(embeddings, labels, source_id):
    layout = Layout(lax.axis_size("row"), lax.axis_size("col"))
    places = layout.places
    samples, width = embeddings.shape
    chunks = width // LANES
    per_peer = samples // layout.devices
    half_count = samples * layout.devices // 2
    factor = 1000.0 / half_count
    tiles = -(-samples // LANES)
    pack_rows = samples * chunks + tiles * SUBLANES
    key_rows = (CORES + FAR_BLOCKS) * samples
    query_rows = places * samples
    block_bytes = pack_rows * LANES * 4
    work_bytes = (key_rows + query_rows) * width * 6 + 8 * GROUP_ROWS * key_rows * 4
    params = pltpu.CompilerParams(vmem_limit_bytes=work_bytes + 4 * MIB)

    packed, ids = pl.pallas_call(
        pack_kernel,
        out_shape=(
            pltpu.VMEM((pack_rows, LANES), jnp.float32),
            pltpu.VMEM((1, samples), jnp.int32),
        ),
        in_specs=[pl.BlockSpec(memory_space=pl.ANY)] * 3,
        out_specs=tuple(vmem_specs(2)),
        scratch_shapes=[
            pltpu.VMEM((1, samples), jnp.int32),
            pltpu.SemaphoreType.DMA((chunks + 2,)),
        ],
        compiler_params=pltpu.CompilerParams(vmem_limit_bytes=4 * block_bytes + 4 * MIB),
        name="pack_block",
    )(
        in_hbm(embeddings),
        in_hbm(labels.reshape(1, samples)),
        in_hbm(source_id.reshape(1, samples)),
    )

    def send(block, target):
        return lax.ppermute(block, ("row", "col"), layout.pairs(target))

    def round_a(plane, place, core):
        return (ROUND_A[plane], place, core)

    def round_b(plane, place, core):
        return (ROUND_B[plane], place, 1 - core if plane in CROSSING else core)

    def to_place(step):
        return lambda plane, place, core: (plane, place ^ step, core)

    def to_core(plane, place, core):
        return (plane, place, 1 - core)

    in_plane = [send(packed, to_place(step)) for step in range(1, places)]
    far_b = send(packed, round_b)
    far_a = send(packed, round_a)
    far_a_other = send(far_a, to_core)
    late, *_ = lax.optimization_barrier((packed, in_plane[-1], far_a))
    near = send(late, to_core)

    ids, far_b = lax.optimization_barrier((ids, far_b))
    lanes, rows = pl.pallas_call(
        functools.partial(pick_kernel, layout, per_peer, factor),
        out_shape=(
            pltpu.VMEM((LANES, 3 * samples), jnp.bfloat16),
            pltpu.VMEM((samples, 3 * samples), jnp.float32),
        ),
        in_specs=vmem_specs(1),
        out_specs=tuple(vmem_specs(2)),
        compiler_params=pltpu.CompilerParams(vmem_limit_bytes=16 * MIB),
        name="pick_masks",
    )(in_vmem(ids))
    far_b, lanes, rows = lax.optimization_barrier((far_b, lanes, rows))
    blocks = [packed, *in_plane, near, far_a, far_a_other, far_b]

    partial = pl.pallas_call(
        functools.partial(main_kernel, samples, chunks, layout),
        out_shape=pltpu.VMEM((samples, LANES), jnp.float32),
        in_specs=vmem_specs(len(blocks)),
        out_specs=pl.BlockSpec(memory_space=pltpu.VMEM),
        scratch_shapes=[
            pltpu.VMEM((2 * key_rows, width), jnp.bfloat16),
            pltpu.VMEM((2 * query_rows, width), jnp.bfloat16),
            pltpu.VMEM((SUBLANES, query_rows), jnp.float32),
        ],
        compiler_params=params,
        name="kernel_sums",
    )(*[in_vmem(block) for block in blocks])

    got = lax.all_to_all(partial, ("row", "col"), split_axis=0, concat_axis=0, tiled=True)

    proof, mmd = pl.pallas_call(
        functools.partial(last_kernel, layout, per_peer, factor / half_count),
        out_shape=(
            jax.ShapeDtypeStruct((1, samples), jnp.float32),
            jax.ShapeDtypeStruct((1, 1), jnp.float32),
        ),
        in_specs=vmem_specs(3),
        out_specs=tuple(vmem_specs(2)),
        compiler_params=pltpu.CompilerParams(vmem_limit_bytes=16 * MIB),
        name="pick_proof",
    )(in_vmem(got), in_vmem(lanes), in_vmem(rows))
    return proof.reshape(samples), mmd.reshape(())


def solution(mesh):
    return jax.shard_map(
        local,
        mesh=mesh,
        in_specs=(P(("row", "col"), None), P(("row", "col")), P(("row", "col"))),
        out_specs=(P(("row", "col")), P()),
        check_vma=False,
    )
```

```python
import functools

import jax
import jax.numpy as jnp
from jax import lax
from jax.experimental import pallas as pl
from jax.experimental.pallas import tpu as pltpu
from jax.sharding import PartitionSpec as P

LANES = 128
SUBLANES = 8
GROUP_ROWS = 256
PLANES = 4
CORES = 2
ROUND_A = {2: 0, 3: 1, 1: 2, 0: 3}
ROUND_B = {0: 1, 3: 2, 1: 0, 2: 3}
CROSSING = (1, 3)
FAR_BLOCKS = 3
MIB = 1024 * 1024
NT_DIMS = (((1,), (1,)), ((), ()))
NN_DIMS = (((1,), (0,)), ((), ()))


def int_div(value, divisor):
    if divisor & (divisor - 1) == 0:
        return lax.shift_right_logical(value, divisor.bit_length() - 1)
    return value // divisor


def int_mod(value, divisor):
    if divisor & (divisor - 1) == 0:
        return value & (divisor - 1)
    return value % divisor


class Layout:
    def __init__(self, row_count, col_count):
        self.core_in_row = row_count == PLANES * CORES
        self.places = col_count if self.core_in_row else col_count // CORES
        self.devices = row_count * col_count

    def flat(self, plane, place, core):
        if self.core_in_row:
            return (plane * CORES + core) * self.places + place
        return (plane * self.places + place) * CORES + core

    def parts(self, flat):
        if self.core_in_row:
            place, rest = int_mod(flat, self.places), int_div(flat, self.places)
            return int_div(rest, CORES), place, int_mod(rest, CORES)
        core, rest = int_mod(flat, CORES), int_div(flat, CORES)
        return int_div(rest, self.places), int_mod(rest, self.places), core

    def here(self):
        row, col = lax.axis_index("row"), lax.axis_index("col")
        if self.core_in_row:
            return int_div(row, CORES), col, int_mod(row, CORES)
        return row, int_div(col, CORES), int_mod(col, CORES)

    def pairs(self, target):
        result = []
        for plane in range(PLANES):
            for place in range(self.places):
                for core in range(CORES):
                    goal = target(plane, place, core)
                    result.append((self.flat(plane, place, core), self.flat(*goal)))
        return sorted(result)


def split2(value):
    high = value.astype(jnp.bfloat16)
    return high, (value - high.astype(jnp.float32)).astype(jnp.bfloat16)


def split3(value):
    high = value.astype(jnp.bfloat16)
    rest = value - high.astype(jnp.float32)
    mid = rest.astype(jnp.bfloat16)
    low = (rest - mid.astype(jnp.float32)).astype(jnp.bfloat16)
    return high, mid, low


def bf16_dot(left, right, dims):
    return lax.dot_general(left, right, dims, preferred_element_type=jnp.float32)


def pack_kernel(emb_ref, label_ref, id_ref, out_ref, id_out_ref, label_vmem, copied):
    samples, width = emb_ref.shape
    chunks = width // LANES
    copies = [
        pltpu.make_async_copy(
            emb_ref.at[:, pl.ds(chunk * LANES, LANES)],
            out_ref.at[pl.ds(chunk * samples, samples), :],
            copied.at[chunk],
        )
        for chunk in range(chunks)
    ]
    copies.append(pltpu.make_async_copy(label_ref, label_vmem, copied.at[chunks]))
    copies.append(pltpu.make_async_copy(id_ref, id_out_ref, copied.at[chunks + 1]))
    for copy in copies:
        copy.start()
    squares = jnp.zeros((samples, LANES), jnp.float32)
    for chunk in range(chunks):
        copies[chunk].wait()
        value = out_ref[pl.ds(chunk * samples, samples), :]
        squares = squares + value * value
    ones = jnp.ones((SUBLANES, LANES), jnp.bfloat16)
    high, mid, low = (bf16_dot(ones, part, NT_DIMS) for part in split3(squares))
    norm = high + (mid + low)
    copies[chunks].wait()
    sign = (1 - 2 * label_vmem[...]).astype(jnp.float32)
    base = samples * chunks
    row = lax.broadcasted_iota(jnp.int32, (SUBLANES, samples), 0)
    both = jnp.where(row == 0, sign, norm)
    for start in range(0, samples, LANES):
        lanes = min(LANES, samples - start)
        place = base + start // LANES * SUBLANES
        if lanes < LANES:
            out_ref[pl.ds(place, SUBLANES), :] = jnp.zeros((SUBLANES, LANES), jnp.float32)
        out_ref[pl.ds(place, SUBLANES), pl.ds(0, lanes)] = both[:, start : start + lanes]
    copies[chunks + 1].wait()


def stage(ref, scratch, start, middle, samples, chunks):
    for chunk in range(chunks):
        value = ref[pl.ds(chunk * samples, samples), :]
        for offset, piece in zip((0, middle), split2(value)):
            scratch[pl.ds(offset + start, samples), pl.ds(chunk * LANES, LANES)] = piece


def tail_rows(refs, samples, chunks):
    pieces = []
    for ref in refs:
        for start in range(0, samples, LANES):
            lanes = min(LANES, samples - start)
            place = samples * chunks + start // LANES * SUBLANES
            pieces.append(ref[pl.ds(place, SUBLANES), pl.ds(0, lanes)])
    return jnp.concatenate(pieces, axis=1)


def as_columns(rows):
    count = rows.shape[1]
    fill = -count % LANES
    if fill:
        rows = jnp.concatenate([rows, jnp.zeros((SUBLANES, fill), jnp.float32)], axis=1)
    return jnp.transpose(rows)[:count]


def main_kernel(samples, chunks, layout, *refs):
    places = layout.places
    queries = refs[:places]
    keys = (refs[0],) + refs[places : places + 4]
    out_ref, key_parts, query_parts, tail_ref = refs[places + 4 :]
    _, me_place, me_core = layout.here()
    rows = places * samples
    key_rows = len(keys) * samples
    group = min(GROUP_ROWS, rows)
    blocks = group // samples
    near = CORES * samples
    for place, ref in enumerate(queries):
        stage(ref, query_parts, place * samples, rows, samples, chunks)
    for place, ref in enumerate(keys):
        stage(ref, key_parts, place * samples, key_rows, samples, chunks)
    key_tail = as_columns(tail_rows(keys, samples, chunks))
    key_sign, key_norm = key_tail[:, 0:1], key_tail[:, 1:2]
    tail_ref[...] = tail_rows(queries, samples, chunks)
    lane = lax.broadcasted_iota(jnp.int32, (samples, LANES), 1)

    def one_group(index, carry):
        result, total, column = carry
        start = pl.multiple_of(index * group, group)
        both = key_parts[...]
        by_high = bf16_dot(both, query_parts[pl.ds(start, group), :], NT_DIMS)
        by_mid = bf16_dot(both, query_parts[pl.ds(rows + start, group), :], NT_DIMS)
        inner = by_high[:key_rows] + (by_high[key_rows:] + by_mid[:key_rows] + by_mid[key_rows:])
        sign = tail_ref[0:1, pl.ds(start, group)]
        norm = tail_ref[1:2, pl.ds(start, group)]
        sq_dist = norm + key_norm - 2.0 * inner
        kernel = jnp.exp(sq_dist * (-1.0 / 200.0))
        signed = kernel * key_sign
        near_sums = jnp.sum(signed[:near], axis=0, keepdims=True)
        far_sums = jnp.sum(signed[near:], axis=0, keepdims=True)
        sums = near_sums + far_sums
        total = total + jnp.sum(sign * (sums + far_sums), axis=1, keepdims=True)
        column = column + jnp.sum(kernel[near:] * sign, axis=1, keepdims=True)
        sums = as_columns(jnp.broadcast_to(sums, (SUBLANES, group)))
        for place in range(blocks):
            owner = me_place ^ (index * blocks + place)
            result = jnp.where(
                lane == owner, sums[place * samples : (place + 1) * samples, 0:1], result
            )
        return result, total, column

    carry = (
        jnp.zeros((samples, LANES), jnp.float32),
        jnp.zeros((1, 1), jnp.float32),
        jnp.zeros((FAR_BLOCKS * samples, 1), jnp.float32),
    )
    if rows == group:
        carry = one_group(0, carry)
    else:
        carry = lax.fori_loop(0, rows // group, one_group, carry)
    result, total, column = carry
    for place, offset in enumerate((me_core, 1 - me_core, 2)):
        result = jnp.where(
            lane == places + offset, column[place * samples : (place + 1) * samples], result
        )
    out_ref[...] = jnp.where(lane == places + 4, total, result)


def pick_kernel(layout, per_peer, factor, id_ref, lane_ref, row_ref):
    ids = id_ref[...]
    samples = ids.shape[1]
    places = layout.places
    plane, place, core = layout.parts(int_div(ids, samples))
    slot = int_mod(ids, per_peer)
    targets = jnp.concatenate(
        [place, places + core, jnp.full(core.shape, places + 2, jnp.int32)], axis=1
    )
    lane_of = lax.broadcasted_iota(jnp.int32, (LANES, 3 * samples), 0)
    lane_ref[...] = jnp.where(lane_of == targets, 1.0, 0.0).astype(jnp.bfloat16)
    row = lax.broadcasted_iota(jnp.int32, (samples, samples), 0)
    src_plane, src_place, src_core = layout.parts(int_div(row, per_peer))
    right_slot = int_mod(row, per_peer) == slot
    right_place = right_slot & (src_place == place)

    def sent_to(table):
        goal = jnp.full(plane.shape, -1, jnp.int32)
        for source, target in table.items():
            goal = jnp.where(plane == source, target, goal)
        return goal

    keep_row = right_slot & (src_plane == plane) & (src_core == core)
    keep_a = right_place & (src_plane == sent_to(ROUND_A))
    crossing = (plane == CROSSING[0]) | (plane == CROSSING[1])
    keep_b = right_place & (src_plane == sent_to(ROUND_B))
    keep_b = keep_b & (src_core == jnp.where(crossing, 1 - core, core))
    row_ref[...] = jnp.concatenate(
        [jnp.where(keep, factor, 0.0) for keep in (keep_row, keep_a, keep_b)], axis=1
    )


def last_kernel(layout, per_peer, scale, got_ref, lane_ref, row_ref, proof_ref, mmd_ref):
    got = got_ref[...]
    samples = got.shape[0]
    parts = jnp.concatenate(split3(got), axis=0)
    picked = bf16_dot(parts, lane_ref[...], NN_DIMS)
    picked = picked[:samples] + (picked[samples : 2 * samples] + picked[2 * samples :])
    sums = jnp.sum(picked * row_ref[...], axis=0, keepdims=True)
    proof_ref[...] = (
        sums[:, :samples] + sums[:, samples : 2 * samples] + sums[:, 2 * samples :]
    )
    row = lax.broadcasted_iota(jnp.int32, (samples, LANES), 0)
    lane = lax.broadcasted_iota(jnp.int32, (samples, LANES), 1)
    is_total = (lane == layout.places + 4) & (int_mod(row, per_peer) == 0)
    total = jnp.sum(jnp.where(is_total, got, 0.0), axis=(0, 1), keepdims=True)
    mmd_ref[...] = total * scale


def in_vmem(array):
    return pltpu.with_memory_space_constraint(array, pltpu.VMEM)


def in_hbm(array):
    return pltpu.with_memory_space_constraint(array, pltpu.HBM)


def vmem_specs(count):
    return [pl.BlockSpec(memory_space=pltpu.VMEM)] * count


def local(embeddings, labels, source_id):
    layout = Layout(lax.axis_size("row"), lax.axis_size("col"))
    places = layout.places
    samples, width = embeddings.shape
    chunks = width // LANES
    per_peer = samples // layout.devices
    half_count = samples * layout.devices // 2
    factor = 1000.0 / half_count
    tiles = -(-samples // LANES)
    pack_rows = samples * chunks + tiles * SUBLANES
    key_rows = (CORES + FAR_BLOCKS) * samples
    query_rows = places * samples
    block_bytes = pack_rows * LANES * 4
    work_bytes = (key_rows + query_rows) * width * 6 + 8 * GROUP_ROWS * key_rows * 4
    params = pltpu.CompilerParams(vmem_limit_bytes=work_bytes + 4 * MIB)

    packed, ids = pl.pallas_call(
        pack_kernel,
        out_shape=(
            pltpu.VMEM((pack_rows, LANES), jnp.float32),
            pltpu.VMEM((1, samples), jnp.int32),
        ),
        in_specs=[pl.BlockSpec(memory_space=pl.ANY)] * 3,
        out_specs=tuple(vmem_specs(2)),
        scratch_shapes=[
            pltpu.VMEM((1, samples), jnp.int32),
            pltpu.SemaphoreType.DMA((chunks + 2,)),
        ],
        compiler_params=pltpu.CompilerParams(vmem_limit_bytes=4 * block_bytes + 4 * MIB),
        name="pack_block",
    )(
        in_hbm(embeddings),
        in_hbm(labels.reshape(1, samples)),
        in_hbm(source_id.reshape(1, samples)),
    )

    def send(block, target):
        return lax.ppermute(block, ("row", "col"), layout.pairs(target))

    def round_a(plane, place, core):
        return (ROUND_A[plane], place, core)

    def round_b(plane, place, core):
        return (ROUND_B[plane], place, 1 - core if plane in CROSSING else core)

    def to_place(step):
        return lambda plane, place, core: (plane, place ^ step, core)

    def to_core(plane, place, core):
        return (plane, place, 1 - core)

    in_plane = [send(packed, to_place(step)) for step in range(1, places)]
    far_b = send(packed, round_b)
    far_a = send(packed, round_a)
    far_a_other = send(far_a, to_core)
    late, *_ = lax.optimization_barrier((packed, in_plane[-1], far_a))
    near = send(late, to_core)

    ids, far_b, *_ = lax.optimization_barrier((ids, far_b, in_plane[0]))
    lanes, rows = pl.pallas_call(
        functools.partial(pick_kernel, layout, per_peer, factor),
        out_shape=(
            pltpu.VMEM((LANES, 3 * samples), jnp.bfloat16),
            pltpu.VMEM((samples, 3 * samples), jnp.float32),
        ),
        in_specs=vmem_specs(1),
        out_specs=tuple(vmem_specs(2)),
        compiler_params=pltpu.CompilerParams(vmem_limit_bytes=16 * MIB),
        name="pick_masks",
    )(in_vmem(ids))
    far_b, lanes, rows = lax.optimization_barrier((far_b, lanes, rows))
    blocks = [packed, *in_plane, near, far_a, far_a_other, far_b]

    partial = pl.pallas_call(
        functools.partial(main_kernel, samples, chunks, layout),
        out_shape=pltpu.VMEM((samples, LANES), jnp.float32),
        in_specs=vmem_specs(len(blocks)),
        out_specs=pl.BlockSpec(memory_space=pltpu.VMEM),
        scratch_shapes=[
            pltpu.VMEM((2 * key_rows, width), jnp.bfloat16),
            pltpu.VMEM((2 * query_rows, width), jnp.bfloat16),
            pltpu.VMEM((SUBLANES, query_rows), jnp.float32),
        ],
        compiler_params=params,
        name="kernel_sums",
    )(*[in_vmem(block) for block in blocks])

    got = lax.all_to_all(partial, ("row", "col"), split_axis=0, concat_axis=0, tiled=True)

    proof, mmd = pl.pallas_call(
        functools.partial(last_kernel, layout, per_peer, factor / half_count),
        out_shape=(
            jax.ShapeDtypeStruct((1, samples), jnp.float32),
            jax.ShapeDtypeStruct((1, 1), jnp.float32),
        ),
        in_specs=vmem_specs(3),
        out_specs=tuple(vmem_specs(2)),
        compiler_params=pltpu.CompilerParams(vmem_limit_bytes=16 * MIB),
        name="pick_proof",
    )(in_vmem(got), in_vmem(lanes), in_vmem(rows))
    return proof.reshape(samples), mmd.reshape(())


def solution(mesh):
    return jax.shard_map(
        local,
        mesh=mesh,
        in_specs=(P(("row", "col"), None), P(("row", "col")), P(("row", "col"))),
        out_specs=(P(("row", "col")), P()),
        check_vma=False,
    )
```
